32 devices in a mesh: dom: 2 (over x), energy: 16 (over z, y, core).
Axes of the slice: x: 2, y: 2, z: 4, core: 2. Of those that a mesh axis runs over, the one named last changes fastest.
Arguments:
- lesser: bfloat16 [1024, 2, 128, 128], P(('dom', 'energy')), parts along dimension 0, may hold values from -6 to 6
- greater: bfloat16 [1024, 2, 128, 128], P(('dom', 'energy')), parts along dimension 0, may hold values from -6 to 6
- dipole: bfloat16 [2, 128, 128], replicated, may hold values from -0.375 to 0.375
- shifts: int32 [16], replicated, may hold values from 1 to 64, as said below
- window: int32 [4], P('dom'), parts along dimension 0, may hold values from 0 to 512, as said below
Outputs:
- polarization: float32 [256, 16, 2, 128], P(('dom', 'energy')), parts along dimension 0
The draws below stay inside these ranges and needn't reach their ends.
There are 2 independent parts, one for each index of `dom`. The reference program is written for one: setup_inputs(seed, part) draws one part's arguments, and reference() takes and returns one part's arrays. A program takes and returns all parts, laid end to end along the dimension named above; an argument that names none is the same for every part. Nothing has to cross between parts.
Inputs may be any that keep to these rules, and one draw needn't show every extreme that they name: `shifts`: every photon energy is at least one bin; one of them is exactly 32 bins and another exactly 64 bins. window[0] < 16 and window[1] >= 384.
All inputs are finite; a program needn't handle non-finite values.
Results may differ from the reference program's by a relative error of at most 0.0029.
Values may be sent and summed in bfloat16 or wider, within the bound.
No kernel may reach another device: no remote copies, remote signals or barrier semaphores. Data moves between devices by JAX's collectives and lax.ppermute only.
A program may use at most 64 MiB of HBM per device.

```python
import math
import jax
import jax.numpy as jnp
from jax import lax

NO = 128
E_DEV = 32
NW = 16
ENERGIES = 512
MAXSHIFT = 64


def draw_shifts(key, part):
    first, second = jax.random.split(jax.random.fold_in(key, 11))
    values = jax.random.randint(first, (NW,), 1, MAXSHIFT)
    order = jax.random.permutation(second, NW)
    place = jnp.arange(NW)
    values = jnp.where(place == order[0], MAXSHIFT, values)
    values = jnp.where(place == order[1], E_DEV, values)
    return values.astype(jnp.int32)


def draw_window(key, part):
    first, second = jax.random.split(jax.random.fold_in(key, 23))
    lower = jax.random.randint(first, (1,), 0, E_DEV // 2)
    upper = jax.random.randint(second, (1,), 3 * ENERGIES // 4, ENERGIES + 1)
    return jnp.concatenate([lower, upper]).astype(jnp.int32)


def block_scale(rng, shape, cuts, least, top_value):
    gain = 1.0
    for position, blocks in cuts:
        draws = jax.random.uniform(jax.random.fold_in(jax.random.fold_in(rng, 6), position), (blocks,), jnp.float32, least / len(cuts), top_value / len(cuts))
        gain = gain * jnp.repeat(jnp.exp(draws), shape[position] // blocks).reshape((-1,) + (1,) * (len(shape) - 1 - position))
    return gain


def noise(key, extent, deviation, most, cuts=(), held_as=jnp.bfloat16):
    array = jax.random.normal(key, extent, jnp.float32) * deviation
    if len(cuts) > 0:
        array = block_scale(key, extent, cuts, -0.22, 0.18) * array
    return jnp.clip(array, min=-most, max=most).astype(held_as)


def setup_inputs(seed: int = 0, part: int = 0) -> dict:
    splits = jax.random.split(jax.random.key(seed), 6)
    own_keys = jax.random.split(jax.random.fold_in(splits[5], part), 6)
    lesser = noise(own_keys[0], (ENERGIES, 2, NO, NO), 1.0, 6.0, ((0, 16),))
    greater = noise(own_keys[1], (ENERGIES, 2, NO, NO), 1.0, 6.0, ((0, 16),))
    dipole = noise(splits[2], (2, NO, NO), (2 * NO) ** -0.5, 0.375)
    shifts = draw_shifts(jax.random.fold_in(splits[5], 71), part)
    window = draw_window(jax.random.fold_in(jax.random.fold_in(splits[5], part), 71), part)
    return {"lesser": lesser, "greater": greater, "dipole": dipole, "shifts": shifts, "window": window}


def reference(lesser, greater, dipole, shifts, window):
    hp = lax.Precision.HIGHEST
    mdip = dipole.astype(jnp.float32)
    mreal, mimag = (mdip[0], mdip[1])
    green = lesser.astype(jnp.float32)
    mg_real = jnp.einsum('ij,ejk->eik', mreal, green[:, 0], precision=hp) - jnp.einsum('ij,ejk->eik', mimag, green[:, 1], precision=hp)
    mg_imag = jnp.einsum('ij,ejk->eik', mreal, green[:, 1], precision=hp) + jnp.einsum('ij,ejk->eik', mimag, green[:, 0], precision=hp)
    c_real = jnp.einsum('eij,kj->eik', mg_real, mreal, precision=hp) + jnp.einsum('eij,kj->eik', mg_imag, mimag, precision=hp)
    c_imag = jnp.einsum('eij,kj->eik', mg_imag, mreal, precision=hp) - jnp.einsum('eij,kj->eik', mg_real, mimag, precision=hp)
    energy = jnp.arange(ENERGIES).astype(jnp.int32)
    inside = ((energy >= window[0]) & (energy < window[1])).astype(jnp.float32)[:, None, None, None]
    projected = jnp.stack([c_real, c_imag], 1).astype(jnp.bfloat16).astype(jnp.float32) * inside
    masked = greater.astype(jnp.float32) * inside
    padded = jnp.concatenate([jnp.zeros((MAXSHIFT, 2, NO, NO), jnp.float32), masked], 0)

    def single(shift_bins):
        start = (MAXSHIFT - shift_bins).astype(jnp.int32)
        part = lax.dynamic_slice_in_dim(padded, start, ENERGIES, 0)
        real = jnp.einsum('eij,ejk->ik', projected[:, 0], part[:, 0], precision=hp) - jnp.einsum('eij,ejk->ik', projected[:, 1], part[:, 1], precision=hp)
        imag = jnp.einsum('eij,ejk->ik', projected[:, 0], part[:, 1], precision=hp) + jnp.einsum('eij,ejk->ik', projected[:, 1], part[:, 0], precision=hp)
        return jnp.stack([real, imag], 0)
    polar = lax.map(single, shifts)
    scale = 1.0 / math.sqrt(2.0 * NO * ENERGIES)
    return jnp.transpose(polar, (2, 0, 1, 3)) * scale
```

```python
import functools
import math

import jax
import jax.numpy as jnp
from jax import lax
from jax.experimental import pallas as pl
from jax.experimental.pallas import tpu as pltpu
from jax.sharding import PartitionSpec as P

STEP = 8
PAIR = 2
PARTS = 4
MIB = 1 << 20


def rotated(real, imag):
    top = jnp.concatenate([real, imag], 1)
    bottom = jnp.concatenate([-imag, real], 1)
    return jnp.concatenate([top, bottom], 0)


def project_kernel(left_ref, right_ref, lesser_ref, out_ref):
    left = left_ref[...]
    right = right_ref[...]
    for u in range(lesser_ref.shape[0]):
        block = rotated(lesser_ref[u, 0], lesser_ref[u, 1])
        inner = jnp.dot(left, block, preferred_element_type=jnp.float32)
        high = inner.astype(jnp.bfloat16)
        low = (inner - high.astype(jnp.float32)).astype(jnp.bfloat16)
        outer = jnp.dot(high, right, preferred_element_type=jnp.float32)
        outer += jnp.dot(low, right, preferred_element_type=jnp.float32)
        out_ref[u] = outer.astype(jnp.bfloat16)


def project(left, right, lesser):
    energies, _, orbitals, _ = lesser.shape
    width = 2 * orbitals
    flops = energies * 2 * orbitals * width * width * 3
    return pl.pallas_call(
        project_kernel,
        out_shape=jax.ShapeDtypeStruct((energies, orbitals, width), jnp.bfloat16),
        grid=(energies // STEP,),
        in_specs=[
            pl.BlockSpec((orbitals, width), lambda t: (0, 0)),
            pl.BlockSpec((width, width), lambda t: (0, 0)),
            pl.BlockSpec((STEP, 2, orbitals, orbitals), lambda t: (t, 0, 0, 0)),
        ],
        out_specs=pl.BlockSpec((STEP, orbitals, width), lambda t: (t, 0, 0)),
        compiler_params=pltpu.CompilerParams(vmem_limit_bytes=16 * MIB),
        cost_estimate=pl.CostEstimate(
            flops=flops, bytes_accessed=lesser.size * 4, transcendentals=0
        ),
    )(left, right, lesser)


def add_products(place_ref, proj_ref, green_ref, total_ref):
    first = pl.program_id(0) * STEP
    photons, rows, width = total_ref.shape
    for w in range(0, photons, PAIR):
        total = total_ref[w : w + PAIR].reshape(PAIR * rows, width)
        for u in range(STEP):
            left = jnp.concatenate(
                [proj_ref[place_ref[first + u, w + v]] for v in range(PAIR)], 0
            )
            right = rotated(green_ref[u, 0], green_ref[u, 1])
            total += jnp.dot(left, right, preferred_element_type=jnp.float32)
        total_ref[w : w + PAIR] = total.reshape(PAIR, rows, width)


def first_kernel(place_ref, proj_ref, green_ref, total_ref):
    @pl.when(pl.program_id(0) == 0)
    def _():
        total_ref[...] = jnp.zeros_like(total_ref)

    add_products(place_ref, proj_ref, green_ref, total_ref)


def next_kernel(place_ref, proj_ref, green_ref, before_ref, total_ref):
    @pl.when(pl.program_id(0) == 0)
    def _():
        total_ref[...] = before_ref[...]

    add_products(place_ref, proj_ref, green_ref, total_ref)


def last_kernel(place_ref, core_ref, proj_ref, green_ref, before_ref, keep_ref, send_ref, total_ref):
    @pl.when(pl.program_id(0) == 0)
    def _():
        total_ref[...] = before_ref[...]

    add_products(place_ref, proj_ref, green_ref, total_ref)

    @pl.when(pl.program_id(0) == pl.num_programs(0) - 1)
    def _():
        half = keep_ref.shape[1]
        core = core_ref[0]
        own = pl.multiple_of(core * half, half)
        other = pl.multiple_of((1 - core) * half, half)
        keep_ref[...] = total_ref[:, pl.ds(own, half), :]
        send_ref[...] = total_ref[:, pl.ds(other, half), :].astype(send_ref.dtype)


def products(place, proj, green, before=None, core=None):
    slots, rows, width = proj.shape
    energies, _, orbitals, _ = green.shape
    photons = place.shape[1]
    smem = pl.BlockSpec(memory_space=pltpu.SMEM)
    total_spec = pl.BlockSpec((photons, rows, width), lambda t: (0, 0, 0))
    total_shape = jax.ShapeDtypeStruct((photons, rows, width), jnp.float32)
    operands, specs = [place], [smem]
    if core is not None:
        operands.append(core)
        specs.append(smem)
    operands += [proj, green]
    specs += [
        pl.BlockSpec((slots, rows, width), lambda t: (0, 0, 0), pipeline_mode=pl.Buffered(1)),
        pl.BlockSpec((STEP, 2, orbitals, orbitals), lambda t: (t, 0, 0, 0)),
    ]
    if before is not None:
        operands.append(before)
        specs.append(
            pl.BlockSpec((photons, rows, width), lambda t: (0, 0, 0), pipeline_mode=pl.Buffered(1))
        )
    scratch = []
    if core is not None:
        half = rows // 2
        half_spec = pl.BlockSpec((photons, half, width), lambda t: (0, 0, 0))
        kernel = last_kernel
        out_specs = [half_spec, half_spec]
        out_shape = [
            jax.ShapeDtypeStruct((photons, half, width), jnp.float32),
            jax.ShapeDtypeStruct((photons, half, width), jnp.bfloat16),
        ]
        scratch = [pltpu.VMEM((photons, rows, width), jnp.float32)]
    else:
        kernel = first_kernel if before is None else next_kernel
        out_specs, out_shape = total_spec, total_shape
    flops = 2 * energies * photons * rows * width * width
    return pl.pallas_call(
        kernel,
        out_shape=out_shape,
        grid=(energies // STEP,),
        in_specs=specs,
        out_specs=out_specs,
        scratch_shapes=scratch,
        compiler_params=pltpu.CompilerParams(vmem_limit_bytes=24 * MIB),
        cost_estimate=pl.CostEstimate(
            flops=flops,
            bytes_accessed=2 * proj.size + 2 * green.size + 8 * photons * rows * width,
            transcendentals=0,
        ),
    )(*operands)


def places(shifts, window, first_energy, core, e_dev):
    zero_slot = 2 * e_dev
    offset = jnp.arange(e_dev, dtype=jnp.int32)[:, None]
    reach = offset + shifts[None, :]
    limit = jnp.where(core == 0, 2 * e_dev, e_dev)

    def inside(energy):
        return (energy >= window[0]) & (energy < window[1])

    own = first_energy + offset
    near = inside(own) & inside(own + shifts[None, :]) & (reach < limit)
    far = inside(own - 2 * e_dev) & inside(own - 2 * e_dev + shifts[None, :]) & (reach >= limit)
    wrapped = jnp.where(reach >= 2 * e_dev, reach - 2 * e_dev, reach)
    return jnp.where(near, reach, zero_slot), jnp.where(far, wrapped, zero_slot)


def on_device(lesser, greater, dipole, shifts, window):
    e_dev, _, orbitals, _ = lesser.shape
    photons = shifts.shape[0]
    devices = lax.axis_size("energy")
    index = lax.axis_index("energy")
    core = index % 2
    chips = devices // 2
    share = orbitals // devices
    total = e_dev * devices

    up = [(i, i + 2) for i in range(devices - 2)]
    across = [(i, i ^ 1) for i in range(devices)]
    piece = e_dev // PARTS
    far = [
        lax.ppermute(greater[k * piece : (k + 1) * piece], "energy", up) for k in range(PARTS)
    ]

    rows = dipole.reshape(2, chips, 2, share, orbitals)
    rows = jnp.transpose(rows, (0, 2, 1, 3, 4)).reshape(2, orbitals, orbitals)
    left = jnp.concatenate([rows[0], rows[1]], 1)
    real, imag = dipole[0].T, dipole[1].T
    right = jnp.concatenate(
        [jnp.concatenate([real, -imag], 1), jnp.concatenate([imag, real], 1)], 0
    )
    proj = project(left, right, lesser)
    other = lax.ppermute(proj, "energy", across)
    zeros = jnp.zeros((1,) + proj.shape[1:], proj.dtype)
    proj = jnp.concatenate([proj, other, zeros], 0)

    near_place, far_place = places(shifts, window, index * e_dev, core, e_dev)
    result = products(near_place, proj, greater)
    for k in range(PARTS):
        place = far_place[k * piece : (k + 1) * piece]
        if k < PARTS - 1:
            result = products(place, proj, far[k], before=result)
    keep, send = products(
        place, proj, far[-1], before=result, core=jnp.reshape(core, (1,)).astype(jnp.int32)
    )
    got = lax.ppermute(send, "energy", across)
    chip_sum = keep + got.astype(jnp.float32)
    chip_sum = chip_sum.reshape(photons, chips, share, 2 * orbitals)
    chip_sum = jnp.transpose(chip_sum, (1, 0, 2, 3)).astype(jnp.bfloat16)
    groups = [[i for i in range(devices) if i % 2 == c] for c in range(2)]
    shares = lax.all_to_all(chip_sum, "energy", 0, 0, axis_index_groups=groups, tiled=True)
    scale = 1.0 / math.sqrt(2.0 * orbitals * total)
    summed = jnp.sum(shares.astype(jnp.float32), 0) * scale
    summed = jnp.transpose(summed, (1, 0, 2))
    return summed.reshape(share, photons, 2, orbitals)


def solution(mesh):
    placed = (
        P(("dom", "energy"), None, None, None),
        P(("dom", "energy"), None, None, None),
        P(),
        P(),
        P("dom"),
    )
    return jax.shard_map(
        on_device,
        mesh=mesh,
        in_specs=placed,
        out_specs=P(("dom", "energy"), None, None, None),
        check_vma=False,
    )
```

```python
import functools
import math

import jax
import jax.numpy as jnp
from jax import lax
from jax.experimental import pallas as pl
from jax.experimental.pallas import tpu as pltpu
from jax.sharding import PartitionSpec as P

STEP = 8
PAIR = 2
PARTS = 4
MIB = 1 << 20


def rotated(real, imag):
    top = jnp.concatenate([real, imag], 1)
    bottom = jnp.concatenate([-imag, real], 1)
    return jnp.concatenate([top, bottom], 0)


def project_blocks(left, right, lesser_ref, out_ref):
    count, rows, width = out_ref.shape
    inner = [
        jnp.dot(
            left,
            rotated(lesser_ref[u, 0], lesser_ref[u, 1]),
            preferred_element_type=jnp.float32,
        )
        for u in range(count)
    ]
    inner = jnp.concatenate(inner, 0)
    high = inner.astype(jnp.bfloat16)
    low = (inner - high.astype(jnp.float32)).astype(jnp.bfloat16)
    outer = jnp.dot(high, right, preferred_element_type=jnp.float32)
    outer += jnp.dot(low, right, preferred_element_type=jnp.float32)
    out_ref[...] = outer.astype(jnp.bfloat16).reshape(count, rows, width)


def project_kernel(steps, left_ref, right_ref, own_ref, other_ref, out_ref):
    t = pl.program_id(0)

    @pl.when(t < steps)
    def _():
        project_blocks(left_ref[...], right_ref[...], own_ref, out_ref)

    @pl.when((t >= steps) & (t < 2 * steps))
    def _():
        project_blocks(left_ref[...], right_ref[...], other_ref, out_ref)

    @pl.when(t == 2 * steps)
    def _():
        out_ref[...] = jnp.zeros_like(out_ref)


def project(left, right, own, other):
    energies, _, orbitals, _ = own.shape
    width = 2 * orbitals
    steps = energies // STEP
    slots = 2 * energies + STEP
    return pl.pallas_call(
        functools.partial(project_kernel, steps),
        out_shape=jax.ShapeDtypeStruct((slots, orbitals, width), jnp.bfloat16),
        grid=(2 * steps + 1,),
        in_specs=[
            pl.BlockSpec((orbitals, width), lambda t: (0, 0)),
            pl.BlockSpec((width, width), lambda t: (0, 0)),
            pl.BlockSpec(
                (STEP, 2, orbitals, orbitals), lambda t: (jnp.minimum(t, steps - 1), 0, 0, 0)
            ),
            pl.BlockSpec(
                (STEP, 2, orbitals, orbitals),
                lambda t: (jnp.clip(t - steps, 0, steps - 1), 0, 0, 0),
            ),
        ],
        out_specs=pl.BlockSpec((STEP, orbitals, width), lambda t: (t, 0, 0)),
        compiler_params=pltpu.CompilerParams(vmem_limit_bytes=16 * MIB),
    )(left, right, own, other)


def add_products(place_ref, proj_ref, green_ref, total_ref):
    first = pl.program_id(0) * STEP
    photons, rows, width = total_ref.shape
    for w in range(0, photons, PAIR):
        total = total_ref[w : w + PAIR].reshape(PAIR * rows, width)
        for u in range(STEP):
            left = jnp.concatenate(
                [proj_ref[place_ref[first + u, w + v]] for v in range(PAIR)], 0
            )
            right = rotated(green_ref[u, 0], green_ref[u, 1])
            total += jnp.dot(left, right, preferred_element_type=jnp.float32)
        total_ref[w : w + PAIR] = total.reshape(PAIR, rows, width)


def first_kernel(place_ref, proj_ref, green_ref, total_ref):
    @pl.when(pl.program_id(0) == 0)
    def _():
        total_ref[...] = jnp.zeros_like(total_ref)

    add_products(place_ref, proj_ref, green_ref, total_ref)


def next_kernel(place_ref, proj_ref, green_ref, before_ref, total_ref):
    @pl.when(pl.program_id(0) == 0)
    def _():
        total_ref[...] = before_ref[...]

    add_products(place_ref, proj_ref, green_ref, total_ref)


def last_kernel(place_ref, core_ref, proj_ref, green_ref, before_ref, keep_ref, send_ref, total_ref):
    @pl.when(pl.program_id(0) == 0)
    def _():
        total_ref[...] = before_ref[...]

    add_products(place_ref, proj_ref, green_ref, total_ref)

    @pl.when(pl.program_id(0) == pl.num_programs(0) - 1)
    def _():
        half = keep_ref.shape[1]
        core = core_ref[0]
        own = pl.multiple_of(core * half, half)
        other = pl.multiple_of((1 - core) * half, half)
        keep_ref[...] = total_ref[:, pl.ds(own, half), :]
        send_ref[...] = total_ref[:, pl.ds(other, half), :].astype(send_ref.dtype)


def products(place, proj, green, before=None, core=None):
    slots, rows, width = proj.shape
    energies, _, orbitals, _ = green.shape
    photons = place.shape[1]
    smem = pl.BlockSpec(memory_space=pltpu.SMEM)
    total_spec = pl.BlockSpec((photons, rows, width), lambda t: (0, 0, 0))
    total_shape = jax.ShapeDtypeStruct((photons, rows, width), jnp.float32)
    operands, specs = [place], [smem]
    if core is not None:
        operands.append(core)
        specs.append(smem)
    operands += [proj, green]
    specs += [
        pl.BlockSpec((slots, rows, width), lambda t: (0, 0, 0), pipeline_mode=pl.Buffered(1)),
        pl.BlockSpec((STEP, 2, orbitals, orbitals), lambda t: (t, 0, 0, 0)),
    ]
    if before is not None:
        operands.append(before)
        specs.append(
            pl.BlockSpec((photons, rows, width), lambda t: (0, 0, 0), pipeline_mode=pl.Buffered(1))
        )
    scratch = []
    if core is not None:
        half = rows // 2
        half_spec = pl.BlockSpec((photons, half, width), lambda t: (0, 0, 0))
        kernel = last_kernel
        out_specs = [half_spec, half_spec]
        out_shape = [
            jax.ShapeDtypeStruct((photons, half, width), jnp.float32),
            jax.ShapeDtypeStruct((photons, half, width), jnp.bfloat16),
        ]
        scratch = [pltpu.VMEM((photons, rows, width), jnp.float32)]
    else:
        kernel = first_kernel if before is None else next_kernel
        out_specs, out_shape = total_spec, total_shape
    return pl.pallas_call(
        kernel,
        out_shape=out_shape,
        grid=(energies // STEP,),
        in_specs=specs,
        out_specs=out_specs,
        scratch_shapes=scratch,
        compiler_params=pltpu.CompilerParams(vmem_limit_bytes=24 * MIB),
    )(*operands)


def places(shifts, window, first_energy, core, e_dev):
    zero_slot = 2 * e_dev
    offset = jnp.arange(e_dev, dtype=jnp.int32)[:, None]
    reach = offset + shifts[None, :]
    limit = jnp.where(core == 0, 2 * e_dev, e_dev)

    def inside(energy):
        return (energy >= window[0]) & (energy < window[1])

    own = first_energy + offset
    near = inside(own) & inside(own + shifts[None, :]) & (reach < limit)
    far = inside(own - 2 * e_dev) & inside(own - 2 * e_dev + shifts[None, :]) & (reach >= limit)
    wrapped = jnp.where(reach >= 2 * e_dev, reach - 2 * e_dev, reach)
    return jnp.where(near, reach, zero_slot), jnp.where(far, wrapped, zero_slot)


def on_device(lesser, greater, dipole, shifts, window):
    e_dev, _, orbitals, _ = lesser.shape
    photons = shifts.shape[0]
    devices = lax.axis_size("energy")
    index = lax.axis_index("energy")
    core = index % 2
    chips = devices // 2
    share = orbitals // devices
    total = e_dev * devices

    up = [(i, i + 2) for i in range(devices - 2)]
    across = [(i, i ^ 1) for i in range(devices)]
    piece = e_dev // PARTS
    pieces = [greater[k * piece : (k + 1) * piece] for k in range(PARTS)]
    far = [lax.ppermute(pieces[k], "energy", up) for k in range(2)]

    rows = dipole.reshape(2, chips, 2, share, orbitals)
    rows = jnp.transpose(rows, (0, 2, 1, 3, 4)).reshape(2, orbitals, orbitals)
    left = jnp.concatenate([rows[0], rows[1]], 1)
    real, imag = dipole[0].T, dipole[1].T
    right = jnp.concatenate(
        [jnp.concatenate([real, -imag], 1), jnp.concatenate([imag, real], 1)], 0
    )
    proj = project(left, right, lesser, lax.ppermute(lesser, "energy", across))

    near_place, far_place = places(shifts, window, index * e_dev, core, e_dev)
    result = products(near_place, proj, greater)
    for k in range(PARTS):
        place = far_place[k * piece : (k + 1) * piece]
        if k < PARTS - 1:
            result = products(place, proj, far[k], before=result)
        if k + 2 < PARTS:
            leaving, result = lax.optimization_barrier((pieces[k + 2], result))
            far.append(lax.ppermute(leaving, "energy", up))
    keep, send = products(
        place, proj, far[-1], before=result, core=jnp.reshape(core, (1,)).astype(jnp.int32)
    )
    got = lax.ppermute(send, "energy", across)
    chip_sum = keep + got.astype(jnp.float32)
    chip_sum = chip_sum.reshape(photons, chips, share, 2 * orbitals)
    chip_sum = jnp.transpose(chip_sum, (1, 0, 2, 3)).astype(jnp.bfloat16)
    groups = [[i for i in range(devices) if i % 2 == c] for c in range(2)]
    shares = lax.all_to_all(chip_sum, "energy", 0, 0, axis_index_groups=groups, tiled=True)
    scale = 1.0 / math.sqrt(2.0 * orbitals * total)
    summed = jnp.sum(shares.astype(jnp.float32), 0) * scale
    summed = jnp.transpose(summed, (1, 0, 2))
    return summed.reshape(share, photons, 2, orbitals)


def solution(mesh):
    placed = (
        P(("dom", "energy"), None, None, None),
        P(("dom", "energy"), None, None, None),
        P(),
        P(),
        P("dom"),
    )
    return jax.shard_map(
        on_device,
        mesh=mesh,
        in_specs=placed,
        out_specs=P(("dom", "energy"), None, None, None),
        check_vma=False,
    )
```

```python
import functools
import math

import jax
import jax.numpy as jnp
from jax import lax
from jax.experimental import pallas as pl
from jax.experimental.pallas import tpu as pltpu
from jax.sharding import PartitionSpec as P

STEP = 8
PAIR = 2
PARTS = 4
MIB = 1 << 20


def rotated(real, imag):
    top = jnp.concatenate([real, imag], 1)
    bottom = jnp.concatenate([-imag, real], 1)
    return jnp.concatenate([top, bottom], 0)


def project_blocks(left, right, lesser_ref, out_ref):
    count, rows, width = out_ref.shape
    inner = [
        jnp.dot(
            left,
            rotated(lesser_ref[u, 0], lesser_ref[u, 1]),
            preferred_element_type=jnp.float32,
        )
        for u in range(count)
    ]
    inner = jnp.concatenate(inner, 0)
    high = inner.astype(jnp.bfloat16)
    low = (inner - high.astype(jnp.float32)).astype(jnp.bfloat16)
    outer = jnp.dot(high, right, preferred_element_type=jnp.float32)
    outer += jnp.dot(low, right, preferred_element_type=jnp.float32)
    out_ref[...] = outer.astype(jnp.bfloat16).reshape(count, rows, width)


def project_kernel(steps, left_ref, right_ref, own_ref, other_ref, out_ref):
    t = pl.program_id(0)

    @pl.when(t < steps)
    def _():
        project_blocks(left_ref[...], right_ref[...], own_ref, out_ref)

    @pl.when((t >= steps) & (t < 2 * steps))
    def _():
        project_blocks(left_ref[...], right_ref[...], other_ref, out_ref)

    @pl.when(t == 2 * steps)
    def _():
        out_ref[...] = jnp.zeros_like(out_ref)


def project(left, right, own, other):
    energies, _, orbitals, _ = own.shape
    width = 2 * orbitals
    steps = energies // STEP
    slots = 2 * energies + STEP
    return pl.pallas_call(
        functools.partial(project_kernel, steps),
        out_shape=jax.ShapeDtypeStruct((slots, orbitals, width), jnp.bfloat16),
        grid=(2 * steps + 1,),
        in_specs=[
            pl.BlockSpec((orbitals, width), lambda t: (0, 0)),
            pl.BlockSpec((width, width), lambda t: (0, 0)),
            pl.BlockSpec(
                (STEP, 2, orbitals, orbitals), lambda t: (jnp.minimum(t, steps - 1), 0, 0, 0)
            ),
            pl.BlockSpec(
                (STEP, 2, orbitals, orbitals),
                lambda t: (jnp.clip(t - steps, 0, steps - 1), 0, 0, 0),
            ),
        ],
        out_specs=pl.BlockSpec((STEP, orbitals, width), lambda t: (t, 0, 0)),
        compiler_params=pltpu.CompilerParams(vmem_limit_bytes=16 * MIB),
    )(left, right, own, other)


def add_products(place_ref, proj_ref, green_ref, total_ref):
    first = pl.program_id(0) * STEP
    photons, rows, width = total_ref.shape
    for w in range(0, photons, PAIR):
        total = total_ref[w : w + PAIR].reshape(PAIR * rows, width)
        for u in range(STEP):
            left = jnp.concatenate(
                [proj_ref[place_ref[first + u, w + v]] for v in range(PAIR)], 0
            )
            right = rotated(green_ref[u, 0], green_ref[u, 1])
            total += jnp.dot(left, right, preferred_element_type=jnp.float32)
        total_ref[w : w + PAIR] = total.reshape(PAIR, rows, width)


def first_kernel(place_ref, proj_ref, green_ref, total_ref):
    @pl.when(pl.program_id(0) == 0)
    def _():
        total_ref[...] = jnp.zeros_like(total_ref)

    add_products(place_ref, proj_ref, green_ref, total_ref)


def next_kernel(place_ref, proj_ref, green_ref, before_ref, total_ref):
    @pl.when(pl.program_id(0) == 0)
    def _():
        total_ref[...] = before_ref[...]

    add_products(place_ref, proj_ref, green_ref, total_ref)


def last_kernel(place_ref, core_ref, proj_ref, green_ref, before_ref, keep_ref, send_ref, total_ref):
    @pl.when(pl.program_id(0) == 0)
    def _():
        total_ref[...] = before_ref[...]

    add_products(place_ref, proj_ref, green_ref, total_ref)

    @pl.when(pl.program_id(0) == pl.num_programs(0) - 1)
    def _():
        half = keep_ref.shape[1]
        core = core_ref[0]
        own = pl.multiple_of(core * half, half)
        other = pl.multiple_of((1 - core) * half, half)
        keep_ref[...] = total_ref[:, pl.ds(own, half), :]
        send_ref[...] = total_ref[:, pl.ds(other, half), :].astype(send_ref.dtype)


def products(place, proj, green, before=None, core=None):
    slots, rows, width = proj.shape
    energies, _, orbitals, _ = green.shape
    photons = place.shape[1]
    smem = pl.BlockSpec(memory_space=pltpu.SMEM)
    total_spec = pl.BlockSpec((photons, rows, width), lambda t: (0, 0, 0))
    total_shape = jax.ShapeDtypeStruct((photons, rows, width), jnp.float32)
    operands, specs = [place], [smem]
    if core is not None:
        operands.append(core)
        specs.append(smem)
    operands += [proj, green]
    specs += [
        pl.BlockSpec((slots, rows, width), lambda t: (0, 0, 0), pipeline_mode=pl.Buffered(1)),
        pl.BlockSpec((STEP, 2, orbitals, orbitals), lambda t: (t, 0, 0, 0)),
    ]
    if before is not None:
        operands.append(before)
        specs.append(
            pl.BlockSpec((photons, rows, width), lambda t: (0, 0, 0), pipeline_mode=pl.Buffered(1))
        )
    scratch = []
    if core is not None:
        half = rows // 2
        half_spec = pl.BlockSpec((photons, half, width), lambda t: (0, 0, 0))
        kernel = last_kernel
        out_specs = [half_spec, half_spec]
        out_shape = [
            jax.ShapeDtypeStruct((photons, half, width), jnp.float32),
            jax.ShapeDtypeStruct((photons, half, width), jnp.bfloat16),
        ]
        scratch = [pltpu.VMEM((photons, rows, width), jnp.float32)]
    else:
        kernel = first_kernel if before is None else next_kernel
        out_specs, out_shape = total_spec, total_shape
    return pl.pallas_call(
        kernel,
        out_shape=out_shape,
        grid=(energies // STEP,),
        in_specs=specs,
        out_specs=out_specs,
        scratch_shapes=scratch,
        compiler_params=pltpu.CompilerParams(vmem_limit_bytes=24 * MIB),
    )(*operands)


def places(shifts, window, first_energy, core, e_dev):
    zero_slot = 2 * e_dev
    offset = jnp.arange(e_dev, dtype=jnp.int32)[:, None]
    reach = offset + shifts[None, :]
    limit = jnp.where(core == 0, 2 * e_dev, e_dev)

    def inside(energy):
        return (energy >= window[0]) & (energy < window[1])

    own = first_energy + offset
    near = inside(own) & inside(own + shifts[None, :]) & (reach < limit)
    far = inside(own - 2 * e_dev) & inside(own - 2 * e_dev + shifts[None, :]) & (reach >= limit)
    wrapped = jnp.where(reach >= 2 * e_dev, reach - 2 * e_dev, reach)
    return jnp.where(near, reach, zero_slot), jnp.where(far, wrapped, zero_slot)


def on_device(lesser, greater, dipole, shifts, window):
    e_dev, _, orbitals, _ = lesser.shape
    photons = shifts.shape[0]
    devices = lax.axis_size("energy")
    index = lax.axis_index("energy")
    core = index % 2
    chips = devices // 2
    share = orbitals // devices
    total = e_dev * devices

    up = [(i, i + 2) for i in range(devices - 2)]
    across = [(i, i ^ 1) for i in range(devices)]
    piece = e_dev // PARTS
    pieces = []
    for k in range(PARTS):
        source = lax.optimization_barrier(greater) if k else greater
        pieces.append(source[k * piece : (k + 1) * piece])
    far = [lax.ppermute(block, "energy", up) for block in pieces[:-1]]

    rows = dipole.reshape(2, chips, 2, share, orbitals)
    rows = jnp.transpose(rows, (0, 2, 1, 3, 4)).reshape(2, orbitals, orbitals)
    left = jnp.concatenate([rows[0], rows[1]], 1)
    real, imag = dipole[0].T, dipole[1].T
    right = jnp.concatenate(
        [jnp.concatenate([real, -imag], 1), jnp.concatenate([imag, real], 1)], 0
    )
    proj = project(left, right, lesser, lax.ppermute(lesser, "energy", across))

    near_place, far_place = places(shifts, window, index * e_dev, core, e_dev)
    result = products(near_place, proj, greater)
    for k in range(PARTS):
        place = far_place[k * piece : (k + 1) * piece]
        if k < PARTS - 1:
            result = products(place, proj, far[k], before=result)
        if k == 0:
            leaving, result = lax.optimization_barrier((pieces[-1], result))
            far.append(lax.ppermute(leaving, "energy", up))
    keep, send = products(
        place, proj, far[-1], before=result, core=jnp.reshape(core, (1,)).astype(jnp.int32)
    )
    got = lax.ppermute(send, "energy", across)
    chip_sum = keep + got.astype(jnp.float32)
    chip_sum = chip_sum.reshape(photons, chips, share, 2 * orbitals)
    chip_sum = jnp.transpose(chip_sum, (1, 0, 2, 3)).astype(jnp.bfloat16)
    groups = [[i for i in range(devices) if i % 2 == c] for c in range(2)]
    shares = lax.all_to_all(chip_sum, "energy", 0, 0, axis_index_groups=groups, tiled=True)
    scale = 1.0 / math.sqrt(2.0 * orbitals * total)
    summed = jnp.sum(shares.astype(jnp.float32), 0) * scale
    summed = jnp.transpose(summed, (1, 0, 2))
    return summed.reshape(share, photons, 2, orbitals)


def solution(mesh):
    placed = (
        P(("dom", "energy"), None, None, None),
        P(("dom", "energy"), None, None, None),
        P(),
        P(),
        P("dom"),
    )
    return jax.shard_map(
        on_device,
        mesh=mesh,
        in_specs=placed,
        out_specs=P(("dom", "energy"), None, None, None),
        check_vma=False,
    )
```

```python
import functools
import math

import jax
import jax.numpy as jnp
from jax import lax
from jax.experimental import pallas as pl
from jax.experimental.pallas import tpu as pltpu
from jax.sharding import PartitionSpec as P

STEP = 8
PAIR = 2
PARTS = 4
MIB = 1 << 20


def rotated(real, imag):
    top = jnp.concatenate([real, imag], 1)
    bottom = jnp.concatenate([-imag, real], 1)
    return jnp.concatenate([top, bottom], 0)


def project_blocks(left, right, lesser_ref, out_ref):
    count, rows, width = out_ref.shape
    inner = [
        jnp.dot(
            left,
            rotated(lesser_ref[u, 0], lesser_ref[u, 1]),
            preferred_element_type=jnp.float32,
        )
        for u in range(count)
    ]
    inner = jnp.concatenate(inner, 0)
    high = inner.astype(jnp.bfloat16)
    low = (inner - high.astype(jnp.float32)).astype(jnp.bfloat16)
    outer = jnp.dot(high, right, preferred_element_type=jnp.float32)
    outer += jnp.dot(low, right, preferred_element_type=jnp.float32)
    out_ref[...] = outer.astype(jnp.bfloat16).reshape(count, rows, width)


def project_kernel(steps, left_ref, right_ref, own_ref, other_ref, out_ref):
    t = pl.program_id(0)

    @pl.when(t < steps)
    def _():
        project_blocks(left_ref[...], right_ref[...], own_ref, out_ref)

    @pl.when((t >= steps) & (t < 2 * steps))
    def _():
        project_blocks(left_ref[...], right_ref[...], other_ref, out_ref)

    @pl.when(t == 2 * steps)
    def _():
        out_ref[...] = jnp.zeros_like(out_ref)


def project(left, right, own, other):
    energies, _, orbitals, _ = own.shape
    width = 2 * orbitals
    steps = energies // STEP
    slots = 2 * energies + STEP
    return pl.pallas_call(
        functools.partial(project_kernel, steps),
        out_shape=jax.ShapeDtypeStruct((slots, orbitals, width), jnp.bfloat16),
        grid=(2 * steps + 1,),
        in_specs=[
            pl.BlockSpec((orbitals, width), lambda t: (0, 0)),
            pl.BlockSpec((width, width), lambda t: (0, 0)),
            pl.BlockSpec(
                (STEP, 2, orbitals, orbitals), lambda t: (jnp.minimum(t, steps - 1), 0, 0, 0)
            ),
            pl.BlockSpec(
                (STEP, 2, orbitals, orbitals),
                lambda t: (jnp.clip(t - steps, 0, steps - 1), 0, 0, 0),
            ),
        ],
        out_specs=pl.BlockSpec((STEP, orbitals, width), lambda t: (t, 0, 0)),
        compiler_params=pltpu.CompilerParams(vmem_limit_bytes=16 * MIB),
    )(left, right, own, other)


def add_products(place_ref, proj_ref, green_ref, total_ref):
    first = pl.program_id(0) * STEP
    photons, rows, width = total_ref.shape
    for w in range(0, photons, PAIR):
        total = total_ref[w : w + PAIR].reshape(PAIR * rows, width)
        for u in range(STEP):
            left = jnp.concatenate(
                [proj_ref[place_ref[first + u, w + v]] for v in range(PAIR)], 0
            )
            right = rotated(green_ref[u, 0], green_ref[u, 1])
            total += jnp.dot(left, right, preferred_element_type=jnp.float32)
        total_ref[w : w + PAIR] = total.reshape(PAIR, rows, width)


def first_kernel(place_ref, proj_ref, green_ref, total_ref):
    @pl.when(pl.program_id(0) == 0)
    def _():
        total_ref[...] = jnp.zeros_like(total_ref)

    add_products(place_ref, proj_ref, green_ref, total_ref)


def next_kernel(place_ref, proj_ref, green_ref, before_ref, total_ref):
    @pl.when(pl.program_id(0) == 0)
    def _():
        total_ref[...] = before_ref[...]

    add_products(place_ref, proj_ref, green_ref, total_ref)


def last_kernel(place_ref, core_ref, proj_ref, green_ref, before_ref, keep_ref, send_ref, total_ref):
    @pl.when(pl.program_id(0) == 0)
    def _():
        total_ref[...] = before_ref[...]

    add_products(place_ref, proj_ref, green_ref, total_ref)

    @pl.when(pl.program_id(0) == pl.num_programs(0) - 1)
    def _():
        half = keep_ref.shape[1]
        core = core_ref[0]
        own = pl.multiple_of(core * half, half)
        other = pl.multiple_of((1 - core) * half, half)
        keep_ref[...] = total_ref[:, pl.ds(own, half), :]
        send_ref[...] = total_ref[:, pl.ds(other, half), :].astype(send_ref.dtype)


def products(place, proj, green, before=None, core=None):
    slots, rows, width = proj.shape
    energies, _, orbitals, _ = green.shape
    photons = place.shape[1]
    smem = pl.BlockSpec(memory_space=pltpu.SMEM)
    total_spec = pl.BlockSpec((photons, rows, width), lambda t: (0, 0, 0))
    total_shape = jax.ShapeDtypeStruct((photons, rows, width), jnp.float32)
    operands, specs = [place], [smem]
    if core is not None:
        operands.append(core)
        specs.append(smem)
    operands += [proj, green]
    specs += [
        pl.BlockSpec((slots, rows, width), lambda t: (0, 0, 0), pipeline_mode=pl.Buffered(1)),
        pl.BlockSpec((STEP, 2, orbitals, orbitals), lambda t: (t, 0, 0, 0)),
    ]
    if before is not None:
        operands.append(before)
        specs.append(
            pl.BlockSpec((photons, rows, width), lambda t: (0, 0, 0), pipeline_mode=pl.Buffered(1))
        )
    scratch = []
    if core is not None:
        half = rows // 2
        half_spec = pl.BlockSpec((photons, half, width), lambda t: (0, 0, 0))
        kernel = last_kernel
        out_specs = [half_spec, half_spec]
        out_shape = [
            jax.ShapeDtypeStruct((photons, half, width), jnp.float32),
            jax.ShapeDtypeStruct((photons, half, width), jnp.bfloat16),
        ]
        scratch = [pltpu.VMEM((photons, rows, width), jnp.float32)]
    else:
        kernel = first_kernel if before is None else next_kernel
        out_specs, out_shape = total_spec, total_shape
    return pl.pallas_call(
        kernel,
        out_shape=out_shape,
        grid=(energies // STEP,),
        in_specs=specs,
        out_specs=out_specs,
        scratch_shapes=scratch,
        compiler_params=pltpu.CompilerParams(vmem_limit_bytes=24 * MIB),
    )(*operands)


def places(shifts, window, first_energy, core, e_dev):
    zero_slot = 2 * e_dev
    offset = jnp.arange(e_dev, dtype=jnp.int32)[:, None]
    reach = offset + shifts[None, :]
    limit = jnp.where(core == 0, 2 * e_dev, e_dev)

    def inside(energy):
        return (energy >= window[0]) & (energy < window[1])

    own = first_energy + offset
    near = inside(own) & inside(own + shifts[None, :]) & (reach < limit)
    far = inside(own - 2 * e_dev) & inside(own - 2 * e_dev + shifts[None, :]) & (reach >= limit)
    wrapped = jnp.where(reach >= 2 * e_dev, reach - 2 * e_dev, reach)
    return jnp.where(near, reach, zero_slot), jnp.where(far, wrapped, zero_slot)


def on_device(lesser, greater, dipole, shifts, window):
    e_dev, _, orbitals, _ = lesser.shape
    photons = shifts.shape[0]
    devices = lax.axis_size("energy")
    index = lax.axis_index("energy")
    core = index % 2
    chips = devices // 2
    share = orbitals // devices
    total = e_dev * devices

    up = [(i, i + 2) for i in range(devices - 2)]
    across = [(i, i ^ 1) for i in range(devices)]
    piece = e_dev // PARTS
    pieces = []
    for k in range(PARTS):
        source = lax.optimization_barrier(greater) if k else greater
        pieces.append(source[k * piece : (k + 1) * piece])
    far = [lax.ppermute(block, "energy", up) for block in pieces]

    rows = dipole.reshape(2, chips, 2, share, orbitals)
    rows = jnp.transpose(rows, (0, 2, 1, 3, 4)).reshape(2, orbitals, orbitals)
    left = jnp.concatenate([rows[0], rows[1]], 1)
    real, imag = dipole[0].T, dipole[1].T
    right = jnp.concatenate(
        [jnp.concatenate([real, -imag], 1), jnp.concatenate([imag, real], 1)], 0
    )
    proj = project(left, right, lesser, lax.ppermute(lesser, "energy", across))

    near_place, far_place = places(shifts, window, index * e_dev, core, e_dev)
    result = products(near_place, proj, greater)
    for k in range(PARTS):
        place = far_place[k * piece : (k + 1) * piece]
        if k < PARTS - 1:
            result = products(place, proj, far[k], before=result)
    keep, send = products(
        place, proj, far[-1], before=result, core=jnp.reshape(core, (1,)).astype(jnp.int32)
    )
    got = lax.ppermute(send, "energy", across)
    chip_sum = keep + got.astype(jnp.float32)
    chip_sum = chip_sum.reshape(photons, chips, share, 2 * orbitals)
    chip_sum = jnp.transpose(chip_sum, (1, 0, 2, 3)).astype(jnp.bfloat16)
    groups = [[i for i in range(devices) if i % 2 == c] for c in range(2)]
    shares = lax.all_to_all(chip_sum, "energy", 0, 0, axis_index_groups=groups, tiled=True)
    scale = 1.0 / math.sqrt(2.0 * orbitals * total)
    summed = jnp.sum(shares.astype(jnp.float32), 0) * scale
    summed = jnp.transpose(summed, (1, 0, 2))
    return summed.reshape(share, photons, 2, orbitals)


def solution(mesh):
    placed = (
        P(("dom", "energy"), None, None, None),
        P(("dom", "energy"), None, None, None),
        P(),
        P(),
        P("dom"),
    )
    return jax.shard_map(
        on_device,
        mesh=mesh,
        in_specs=placed,
        out_specs=P(("dom", "energy"), None, None, None),
        check_vma=False,
    )
```

```python
import functools
import math

import jax
import jax.numpy as jnp
from jax import lax
from jax.experimental import pallas as pl
from jax.experimental.pallas import tpu as pltpu
from jax.sharding import PartitionSpec as P

STEP = 8
GROUPS = 2
PARTS = 4
MIB = 1 << 20


def rotated(real, imag):
    top = jnp.concatenate([real, imag], 1)
    bottom = jnp.concatenate([-imag, real], 1)
    return jnp.concatenate([top, bottom], 0)


def project_blocks(left, right, lesser_ref, out_ref):
    count, rows, width = out_ref.shape
    inner = [
        jnp.dot(
            left,
            rotated(lesser_ref[u, 0], lesser_ref[u, 1]),
            preferred_element_type=jnp.float32,
        )
        for u in range(count)
    ]
    inner = jnp.concatenate(inner, 0)
    high = inner.astype(jnp.bfloat16)
    low = (inner - high.astype(jnp.float32)).astype(jnp.bfloat16)
    outer = jnp.dot(high, right, preferred_element_type=jnp.float32)
    outer += jnp.dot(low, right, preferred_element_type=jnp.float32)
    out_ref[...] = outer.astype(jnp.bfloat16).reshape(count, rows, width)


def project_kernel(steps, left_ref, right_ref, own_ref, other_ref, out_ref):
    t = pl.program_id(0)

    @pl.when(t < steps)
    def _():
        project_blocks(left_ref[...], right_ref[...], own_ref, out_ref)

    @pl.when((t >= steps) & (t < 2 * steps))
    def _():
        project_blocks(left_ref[...], right_ref[...], other_ref, out_ref)

    @pl.when(t == 2 * steps)
    def _():
        out_ref[...] = jnp.zeros_like(out_ref)


def project(left, right, own, other):
    energies, _, orbitals, _ = own.shape
    width = 2 * orbitals
    steps = energies // STEP
    slots = 2 * energies + STEP
    return pl.pallas_call(
        functools.partial(project_kernel, steps),
        out_shape=jax.ShapeDtypeStruct((slots, orbitals, width), jnp.bfloat16),
        grid=(2 * steps + 1,),
        in_specs=[
            pl.BlockSpec((orbitals, width), lambda t: (0, 0)),
            pl.BlockSpec((width, width), lambda t: (0, 0)),
            pl.BlockSpec(
                (STEP, 2, orbitals, orbitals), lambda t: (jnp.minimum(t, steps - 1), 0, 0, 0)
            ),
            pl.BlockSpec(
                (STEP, 2, orbitals, orbitals),
                lambda t: (jnp.clip(t - steps, 0, steps - 1), 0, 0, 0),
            ),
        ],
        out_specs=pl.BlockSpec((STEP, orbitals, width), lambda t: (t, 0, 0)),
        compiler_params=pltpu.CompilerParams(vmem_limit_bytes=16 * MIB),
    )(left, right, own, other)


def add_products(reach_ref, place_ref, proj_ref, green_ref, total_ref, start, far):
    first = pl.program_id(0) * STEP
    photons = total_ref.shape[0]
    for w in range(photons):
        lowest = reach_ref[start + w] + first
        limit = reach_ref[reach_ref.shape[0] - 1]
        needed = lowest + STEP - 1 >= limit if far else lowest < limit

        @pl.when(needed)
        def _():
            total = total_ref[w]
            for u in range(STEP):
                right = rotated(green_ref[u, 0], green_ref[u, 1])
                left = proj_ref[place_ref[first + u, start + w]]
                total += jnp.dot(left, right, preferred_element_type=jnp.float32)
            total_ref[w] = total


def near_kernel(reach_ref, place_ref, proj_ref, green_ref, total_ref):
    @pl.when(pl.program_id(0) == 0)
    def _():
        total_ref[...] = jnp.zeros_like(total_ref)

    add_products(reach_ref, place_ref, proj_ref, green_ref, total_ref, 0, False)


def far_kernel(reach_ref, place_ref, proj_ref, green_ref, before_ref, total_ref):
    @pl.when(pl.program_id(0) == 0)
    def _():
        total_ref[...] = before_ref[...]

    add_products(reach_ref, place_ref, proj_ref, green_ref, total_ref, 0, True)


def last_kernel(
    start,
    reach_ref,
    place_ref,
    core_ref,
    proj_ref,
    green_ref,
    before_ref,
    keep_ref,
    send_ref,
    total_ref,
):
    @pl.when(pl.program_id(0) == 0)
    def _():
        total_ref[...] = before_ref[...]

    add_products(reach_ref, place_ref, proj_ref, green_ref, total_ref, start, True)

    @pl.when(pl.program_id(0) == pl.num_programs(0) - 1)
    def _():
        half = keep_ref.shape[1]
        core = core_ref[0]
        own = pl.multiple_of(core * half, half)
        other = pl.multiple_of((1 - core) * half, half)
        keep_ref[...] = total_ref[:, pl.ds(own, half), :]
        send_ref[...] = total_ref[:, pl.ds(other, half), :].astype(send_ref.dtype)


def products(reach, place, proj, green, before=None, core=None, group=0):
    slots, rows, width = proj.shape
    energies, _, orbitals, _ = green.shape
    photons = place.shape[1]
    smem = pl.BlockSpec(memory_space=pltpu.SMEM)
    if core is not None:
        photons //= GROUPS
    block = (photons, rows, width)
    operands, specs = [reach, place], [smem, smem]
    if core is not None:
        operands.append(core)
        specs.append(smem)
    operands += [proj, green]
    specs += [
        pl.BlockSpec((slots, rows, width), lambda t: (0, 0, 0), pipeline_mode=pl.Buffered(1)),
        pl.BlockSpec((STEP, 2, orbitals, orbitals), lambda t: (t, 0, 0, 0)),
    ]
    if before is not None:
        operands.append(before)
        specs.append(
            pl.BlockSpec(block, lambda t: (group, 0, 0), pipeline_mode=pl.Buffered(1))
        )
    scratch = []
    if core is not None:
        half = (photons, rows // 2, width)
        kernel = functools.partial(last_kernel, group * photons)
        out_specs = [pl.BlockSpec(half, lambda t: (0, 0, 0))] * 2
        out_shape = [
            jax.ShapeDtypeStruct(half, jnp.float32),
            jax.ShapeDtypeStruct(half, jnp.bfloat16),
        ]
        scratch = [pltpu.VMEM(block, jnp.float32)]
    else:
        kernel = near_kernel if before is None else far_kernel
        out_specs = pl.BlockSpec(block, lambda t: (0, 0, 0))
        out_shape = jax.ShapeDtypeStruct(block, jnp.float32)
    return pl.pallas_call(
        kernel,
        out_shape=out_shape,
        grid=(energies // STEP,),
        in_specs=specs,
        out_specs=out_specs,
        scratch_shapes=scratch,
        compiler_params=pltpu.CompilerParams(vmem_limit_bytes=24 * MIB),
    )(*operands)


def places(shifts, window, first_energy, core, e_dev):
    zero_slot = 2 * e_dev
    offset = jnp.arange(e_dev, dtype=jnp.int32)[:, None]
    reach = offset + shifts[None, :]
    limit = jnp.where(core == 0, 2 * e_dev, e_dev)

    def inside(energy):
        return (energy >= window[0]) & (energy < window[1])

    own = first_energy + offset
    near = inside(own) & inside(own + shifts[None, :]) & (reach < limit)
    far = inside(own - 2 * e_dev) & inside(own - 2 * e_dev + shifts[None, :]) & (reach >= limit)
    wrapped = jnp.where(reach >= 2 * e_dev, reach - 2 * e_dev, reach)
    return jnp.where(near, reach, zero_slot), jnp.where(far, wrapped, zero_slot)


def pick(blocks, place):
    return lax.dynamic_index_in_dim(blocks, place, 0, keepdims=False)


def reduced(keep, send, planes, share):
    devices = 4 * planes
    index = lax.axis_index("energy")
    plane, chip = index // 4, (index // 2) % 2
    photons, half, width = keep.shape
    got = lax.ppermute(send, "energy", [(i, i ^ 1) for i in range(devices)])
    both = keep + got.astype(jnp.float32)
    both = both.reshape(photons, 2, planes, share, width)
    both = jnp.transpose(both, (1, 2, 0, 3, 4))
    send = pick(both, 1 - chip).astype(jnp.bfloat16)
    got = lax.ppermute(send, "energy", [(i, i ^ 2) for i in range(devices)])
    both = pick(both, chip) + got.astype(jnp.float32)
    total = pick(both, plane)
    for step in range(1, planes):
        send = pick(both, (plane + step) % planes).astype(jnp.bfloat16)
        route = [(i, (i + 4 * step) % devices) for i in range(devices)]
        total = total + lax.ppermute(send, "energy", route).astype(jnp.float32)
    return total


def on_device(lesser, greater, dipole, shifts, window):
    e_dev, _, orbitals, _ = lesser.shape
    photons = shifts.shape[0]
    devices = lax.axis_size("energy")
    index = lax.axis_index("energy")
    core = index % 2
    share = orbitals // devices
    total = e_dev * devices

    up = [(i, i + 2) for i in range(devices - 2)]
    across = [(i, i ^ 1) for i in range(devices)]
    piece = e_dev // PARTS
    pieces = [greater[:piece]]
    lesser, greater, pieces[0] = lax.optimization_barrier((lesser, greater, pieces[0]))
    pieces += [greater[k * piece : (k + 1) * piece] for k in range(1, PARTS)]
    far = [lax.ppermute(block, "energy", up) for block in pieces]

    planes = devices // 4
    rows = dipole.reshape(2, planes, 2, 2, share, orbitals)
    rows = jnp.transpose(rows, (0, 3, 2, 1, 4, 5)).reshape(2, orbitals, orbitals)
    left = jnp.concatenate([rows[0], rows[1]], 1)
    real, imag = dipole[0].T, dipole[1].T
    right = jnp.concatenate(
        [jnp.concatenate([real, -imag], 1), jnp.concatenate([imag, real], 1)], 0
    )
    proj = project(left, right, lesser, lax.ppermute(lesser, "energy", across))

    near_place, far_place = places(shifts, window, index * e_dev, core, e_dev)
    limit = jnp.where(core == 0, 2 * e_dev, e_dev)[None]
    result = products(jnp.concatenate([shifts, limit]), near_place, proj, greater)
    core = core[None]
    for k in range(PARTS):
        place = far_place[k * piece : (k + 1) * piece]
        reach = jnp.concatenate([shifts, limit - k * piece])
        if k < PARTS - 1:
            result = products(reach, place, proj, far[k], before=result)
    sums = []
    for group in range(GROUPS):
        keep, send = products(reach, place, proj, far[-1], before=result, core=core, group=group)
        sums.append(reduced(keep, send, planes, share))
    scale = 1.0 / math.sqrt(2.0 * orbitals * total)
    summed = jnp.concatenate(sums, 0) * scale
    summed = jnp.transpose(summed, (1, 0, 2))
    return summed.reshape(share, photons, 2, orbitals)


def solution(mesh):
    placed = (
        P(("dom", "energy"), None, None, None),
        P(("dom", "energy"), None, None, None),
        P(),
        P(),
        P("dom"),
    )
    return jax.shard_map(
        on_device,
        mesh=mesh,
        in_specs=placed,
        out_specs=P(("dom", "energy"), None, None, None),
        check_vma=False,
    )
```

```python
import functools
import math

import jax
import jax.numpy as jnp
from jax import lax
from jax.experimental import pallas as pl
from jax.experimental.pallas import tpu as pltpu
from jax.sharding import PartitionSpec as P

STEP = 8
PAIR = 2
GROUPS = 1
PARTS = (24, 4, 4)
MIB = 1 << 20


def rotated(real, imag):
    top = jnp.concatenate([real, imag], 1)
    bottom = jnp.concatenate([-imag, real], 1)
    return jnp.concatenate([top, bottom], 0)


def cut_kernel(sizes, source_ref, *refs):
    sems = refs[-1]
    copies = []
    first = 0
    for k, size in enumerate(sizes):
        copies.append(
            pltpu.make_async_copy(source_ref.at[pl.ds(first, size)], refs[k], sems.at[k])
        )
        copies[-1].start()
        first += size
    for copy in copies:
        copy.wait()


def cut(blocks, sizes):
    return pl.pallas_call(
        functools.partial(cut_kernel, sizes),
        out_shape=[jax.ShapeDtypeStruct((size,) + blocks.shape[1:], blocks.dtype) for size in sizes],
        in_specs=[pl.BlockSpec(memory_space=pl.ANY)],
        out_specs=[pl.BlockSpec(memory_space=pl.ANY)] * len(sizes),
        scratch_shapes=[pltpu.SemaphoreType.DMA((len(sizes),))],
    )(blocks)


def project_blocks(left, right, lesser_ref, out_ref):
    count, rows, width = out_ref.shape
    inner = [
        jnp.dot(
            left,
            rotated(lesser_ref[u, 0], lesser_ref[u, 1]),
            preferred_element_type=jnp.float32,
        )
        for u in range(count)
    ]
    inner = jnp.concatenate(inner, 0)
    high = inner.astype(jnp.bfloat16)
    low = (inner - high.astype(jnp.float32)).astype(jnp.bfloat16)
    outer = jnp.dot(high, right, preferred_element_type=jnp.float32)
    outer += jnp.dot(low, right, preferred_element_type=jnp.float32)
    out_ref[...] = outer.astype(jnp.bfloat16).reshape(count, rows, width)


def project_kernel(steps, left_ref, right_ref, own_ref, other_ref, out_ref):
    t = pl.program_id(0)

    @pl.when(t < steps)
    def _():
        project_blocks(left_ref[...], right_ref[...], own_ref, out_ref)

    @pl.when((t >= steps) & (t < 2 * steps))
    def _():
        project_blocks(left_ref[...], right_ref[...], other_ref, out_ref)

    @pl.when(t == 2 * steps)
    def _():
        out_ref[...] = jnp.zeros_like(out_ref)


def project(left, right, own, other):
    energies, _, orbitals, _ = own.shape
    width = 2 * orbitals
    steps = energies // STEP
    slots = 2 * energies + STEP
    return pl.pallas_call(
        functools.partial(project_kernel, steps),
        out_shape=jax.ShapeDtypeStruct((slots, orbitals, width), jnp.bfloat16),
        grid=(2 * steps + 1,),
        in_specs=[
            pl.BlockSpec((orbitals, width), lambda t: (0, 0)),
            pl.BlockSpec((width, width), lambda t: (0, 0)),
            pl.BlockSpec(
                (STEP, 2, orbitals, orbitals), lambda t: (jnp.minimum(t, steps - 1), 0, 0, 0)
            ),
            pl.BlockSpec(
                (STEP, 2, orbitals, orbitals),
                lambda t: (jnp.clip(t - steps, 0, steps - 1), 0, 0, 0),
            ),
        ],
        out_specs=pl.BlockSpec((STEP, orbitals, width), lambda t: (t, 0, 0)),
        compiler_params=pltpu.CompilerParams(vmem_limit_bytes=16 * MIB),
    )(left, right, own, other)


def add_products(place_ref, proj_ref, green_ref, total_ref, start):
    step = green_ref.shape[0]
    first = pl.program_id(0) * step
    photons, rows, width = total_ref.shape
    for w in range(0, photons, PAIR):
        total = total_ref[w : w + PAIR].reshape(PAIR * rows, width)
        for u in range(step):
            left = jnp.concatenate(
                [proj_ref[place_ref[first + u, start + w + v]] for v in range(PAIR)], 0
            )
            right = rotated(green_ref[u, 0], green_ref[u, 1])
            total += jnp.dot(left, right, preferred_element_type=jnp.float32)
        total_ref[w : w + PAIR] = total.reshape(PAIR, rows, width)


def near_kernel(place_ref, proj_ref, green_ref, total_ref):
    @pl.when(pl.program_id(0) == 0)
    def _():
        total_ref[...] = jnp.zeros_like(total_ref)

    add_products(place_ref, proj_ref, green_ref, total_ref, 0)


def far_kernel(place_ref, proj_ref, green_ref, before_ref, total_ref):
    @pl.when(pl.program_id(0) == 0)
    def _():
        total_ref[...] = before_ref[...]

    add_products(place_ref, proj_ref, green_ref, total_ref, 0)


def last_kernel(
    start,
    place_ref,
    core_ref,
    proj_ref,
    green_ref,
    before_ref,
    keep_ref,
    send_ref,
    total_ref,
):
    @pl.when(pl.program_id(0) == 0)
    def _():
        total_ref[...] = before_ref[...]

    add_products(place_ref, proj_ref, green_ref, total_ref, start)

    @pl.when(pl.program_id(0) == pl.num_programs(0) - 1)
    def _():
        half = keep_ref.shape[1]
        core = core_ref[0]
        own = pl.multiple_of(core * half, half)
        other = pl.multiple_of((1 - core) * half, half)
        keep_ref[...] = total_ref[:, pl.ds(own, half), :]
        send_ref[...] = total_ref[:, pl.ds(other, half), :].astype(send_ref.dtype)


def products(place, proj, green, before=None, core=None, group=0):
    slots, rows, width = proj.shape
    energies, _, orbitals, _ = green.shape
    step = min(STEP, energies)
    photons = place.shape[1]
    smem = pl.BlockSpec(memory_space=pltpu.SMEM)
    if core is not None:
        photons //= GROUPS
    block = (photons, rows, width)
    operands, specs = [place], [smem]
    if core is not None:
        operands.append(core)
        specs.append(smem)
    operands += [proj, green]
    specs += [
        pl.BlockSpec((slots, rows, width), lambda t: (0, 0, 0), pipeline_mode=pl.Buffered(1)),
        pl.BlockSpec((step, 2, orbitals, orbitals), lambda t: (t, 0, 0, 0)),
    ]
    if before is not None:
        operands.append(before)
        specs.append(
            pl.BlockSpec(block, lambda t: (group, 0, 0), pipeline_mode=pl.Buffered(1))
        )
    scratch = []
    if core is not None:
        half = (photons, rows // 2, width)
        kernel = functools.partial(last_kernel, group * photons)
        out_specs = [pl.BlockSpec(half, lambda t: (0, 0, 0))] * 2
        out_shape = [
            jax.ShapeDtypeStruct(half, jnp.float32),
            jax.ShapeDtypeStruct(half, jnp.bfloat16),
        ]
        scratch = [pltpu.VMEM(block, jnp.float32)]
    else:
        kernel = near_kernel if before is None else far_kernel
        out_specs = pl.BlockSpec(block, lambda t: (0, 0, 0))
        out_shape = jax.ShapeDtypeStruct(block, jnp.float32)
    return pl.pallas_call(
        kernel,
        out_shape=out_shape,
        grid=(energies // step,),
        in_specs=specs,
        out_specs=out_specs,
        scratch_shapes=scratch,
        compiler_params=pltpu.CompilerParams(vmem_limit_bytes=24 * MIB),
    )(*operands)


def places(shifts, window, first_energy, core, e_dev):
    zero_slot = 2 * e_dev
    offset = jnp.arange(e_dev, dtype=jnp.int32)[:, None]
    reach = offset + shifts[None, :]
    limit = jnp.where(core == 0, 2 * e_dev, e_dev)

    def inside(energy):
        return (energy >= window[0]) & (energy < window[1])

    own = first_energy + offset
    near = inside(own) & inside(own + shifts[None, :]) & (reach < limit)
    far = inside(own - 2 * e_dev) & inside(own - 2 * e_dev + shifts[None, :]) & (reach >= limit)
    wrapped = jnp.where(reach >= 2 * e_dev, reach - 2 * e_dev, reach)
    return jnp.where(near, reach, zero_slot), jnp.where(far, wrapped, zero_slot)


def pick(blocks, place):
    return lax.dynamic_index_in_dim(blocks, place, 0, keepdims=False)


def reduced(keep, send, planes, share):
    devices = 4 * planes
    index = lax.axis_index("energy")
    plane, chip = index // 4, (index // 2) % 2
    photons, half, width = keep.shape
    got = lax.ppermute(send, "energy", [(i, i ^ 1) for i in range(devices)])
    both = keep + got.astype(jnp.float32)
    both = both.reshape(photons, 2, planes, share, width)
    both = jnp.transpose(both, (1, 2, 0, 3, 4))
    send = pick(both, 1 - chip).astype(jnp.bfloat16)
    got = lax.ppermute(send, "energy", [(i, i ^ 2) for i in range(devices)])
    both = pick(both, chip) + got.astype(jnp.float32)
    total = pick(both, plane)
    for step in range(1, planes):
        send = pick(both, (plane + step) % planes).astype(jnp.bfloat16)
        route = [(i, (i + 4 * step) % devices) for i in range(devices)]
        total = total + lax.ppermute(send, "energy", route).astype(jnp.float32)
    return total


def on_device(lesser, greater, dipole, shifts, window):
    e_dev, _, orbitals, _ = lesser.shape
    photons = shifts.shape[0]
    devices = lax.axis_size("energy")
    index = lax.axis_index("energy")
    core = index % 2
    share = orbitals // devices
    total = e_dev * devices

    up = [(i, i + 2) for i in range(devices - 2)]
    across = [(i, i ^ 1) for i in range(devices)]
    sizes = [e_dev * part // 32 for part in PARTS]
    pieces = list(cut(greater, sizes))
    far = [lax.ppermute(pieces[0], "energy", up)]

    planes = devices // 4
    rows = dipole.reshape(2, planes, 2, 2, share, orbitals)
    rows = jnp.transpose(rows, (0, 3, 2, 1, 4, 5)).reshape(2, orbitals, orbitals)
    left = jnp.concatenate([rows[0], rows[1]], 1)
    real, imag = dipole[0].T, dipole[1].T
    right = jnp.concatenate(
        [jnp.concatenate([real, -imag], 1), jnp.concatenate([imag, real], 1)], 0
    )
    proj = project(left, right, lesser, lax.ppermute(lesser, "energy", across))

    pieces[1], proj = lax.optimization_barrier((pieces[1], proj))
    far.append(lax.ppermute(pieces[1], "energy", up))

    near_place, far_place = places(shifts, window, index * e_dev, core, e_dev)
    result = products(near_place, proj, greater)
    pieces[2], result = lax.optimization_barrier((pieces[2], result))
    far.append(lax.ppermute(pieces[2], "energy", up))
    core = core[None]
    first = 0
    for k, size in enumerate(sizes):
        place = far_place[first : first + size]
        first += size
        if k < len(sizes) - 1:
            result = products(place, proj, far[k], before=result)
    sums = []
    for group in range(GROUPS):
        keep, send = products(place, proj, far[-1], before=result, core=core, group=group)
        sums.append(reduced(keep, send, planes, share))
    scale = 1.0 / math.sqrt(2.0 * orbitals * total)
    summed = jnp.concatenate(sums, 0) * scale
    summed = jnp.transpose(summed, (1, 0, 2))
    return summed.reshape(share, photons, 2, orbitals)


def solution(mesh):
    placed = (
        P(("dom", "energy"), None, None, None),
        P(("dom", "energy"), None, None, None),
        P(),
        P(),
        P("dom"),
    )
    return jax.shard_map(
        on_device,
        mesh=mesh,
        in_specs=placed,
        out_specs=P(("dom", "energy"), None, None, None),
        check_vma=False,
    )
```

```python
import functools
import math

import jax
import jax.numpy as jnp
from jax import lax
from jax.experimental import pallas as pl
from jax.experimental.pallas import tpu as pltpu
from jax.sharding import PartitionSpec as P

STEP = 8
WIDE = 16
PAIR = 2
GROUPS = 1
PARTS = (24, 4, 4)
MIB = 1 << 20


def rotated(real, imag):
    top = jnp.concatenate([real, imag], 1)
    bottom = jnp.concatenate([-imag, real], 1)
    return jnp.concatenate([top, bottom], 0)


def cut_kernel(sizes, source_ref, *refs):
    sems = refs[-1]
    copies = []
    first = 0
    for k, size in enumerate(sizes):
        copies.append(
            pltpu.make_async_copy(source_ref.at[pl.ds(first, size)], refs[k], sems.at[k])
        )
        copies[-1].start()
        first += size
    for copy in copies:
        copy.wait()


def cut(blocks, sizes):
    return pl.pallas_call(
        functools.partial(cut_kernel, sizes),
        out_shape=[pltpu.VMEM((size,) + blocks.shape[1:], blocks.dtype) for size in sizes],
        in_specs=[pl.BlockSpec(memory_space=pl.ANY)],
        out_specs=[pl.BlockSpec(memory_space=pltpu.VMEM)] * len(sizes),
        scratch_shapes=[pltpu.SemaphoreType.DMA((len(sizes),))],
        compiler_params=pltpu.CompilerParams(vmem_limit_bytes=8 * MIB),
    )(blocks)


def project_blocks(left, right, lesser_ref, out_ref):
    count, rows, width = out_ref.shape
    inner = [
        jnp.dot(
            left,
            rotated(lesser_ref[u, 0], lesser_ref[u, 1]),
            preferred_element_type=jnp.float32,
        )
        for u in range(count)
    ]
    inner = jnp.concatenate(inner, 0)
    high = inner.astype(jnp.bfloat16)
    low = (inner - high.astype(jnp.float32)).astype(jnp.bfloat16)
    outer = jnp.dot(high, right, preferred_element_type=jnp.float32)
    outer += jnp.dot(low, right, preferred_element_type=jnp.float32)
    out_ref[...] = outer.astype(jnp.bfloat16).reshape(count, rows, width)


def project_kernel(steps, left_ref, right_ref, own_ref, other_ref, out_ref):
    t = pl.program_id(0)

    @pl.when(t < steps)
    def _():
        project_blocks(left_ref[...], right_ref[...], own_ref, out_ref)

    @pl.when((t >= steps) & (t < 2 * steps))
    def _():
        project_blocks(left_ref[...], right_ref[...], other_ref, out_ref)

    @pl.when(t == 2 * steps)
    def _():
        out_ref[...] = jnp.zeros_like(out_ref)


def project(left, right, own, other):
    energies, _, orbitals, _ = own.shape
    width = 2 * orbitals
    steps = energies // WIDE
    slots = 2 * energies + WIDE
    return pl.pallas_call(
        functools.partial(project_kernel, steps),
        out_shape=jax.ShapeDtypeStruct((slots, orbitals, width), jnp.bfloat16),
        grid=(2 * steps + 1,),
        in_specs=[
            pl.BlockSpec((orbitals, width), lambda t: (0, 0)),
            pl.BlockSpec((width, width), lambda t: (0, 0)),
            pl.BlockSpec(
                (WIDE, 2, orbitals, orbitals), lambda t: (jnp.minimum(t, steps - 1), 0, 0, 0)
            ),
            pl.BlockSpec(
                (WIDE, 2, orbitals, orbitals),
                lambda t: (jnp.clip(t - steps, 0, steps - 1), 0, 0, 0),
            ),
        ],
        out_specs=pl.BlockSpec((WIDE, orbitals, width), lambda t: (t, 0, 0)),
        compiler_params=pltpu.CompilerParams(vmem_limit_bytes=16 * MIB),
    )(left, right, own, other)


def pair_place(shift, offset, far, facts_ref, zero_place):
    low, high, base, limit, e_dev = (facts_ref[i] for i in range(5))
    reach = offset + shift
    energy = base + offset
    if far:
        energy = energy - 2 * e_dev
    met = reach >= limit if far else reach < limit
    met = met & (energy >= low) & (energy + shift < high)
    if far:
        reach = jnp.where(reach >= 2 * e_dev, reach - 2 * e_dev, reach)
    return jnp.where(met, reach, zero_place)


def add_products(shifts_ref, facts_ref, proj_ref, green_ref, total_ref, start, far, offset):
    step = green_ref.shape[0]
    first = pl.program_id(0) * step + offset
    photons, rows, width = total_ref.shape
    zero_place = proj_ref.shape[0] - 1
    for w in range(0, photons, PAIR):
        shifts = [shifts_ref[start + w + v] for v in range(PAIR)]
        total = total_ref[w : w + PAIR].reshape(PAIR * rows, width)
        for u in range(step):
            places = [pair_place(shift, first + u, far, facts_ref, zero_place) for shift in shifts]
            left = jnp.concatenate([proj_ref[place] for place in places], 0)
            right = rotated(green_ref[u, 0], green_ref[u, 1])
            total += jnp.dot(left, right, preferred_element_type=jnp.float32)
        total_ref[w : w + PAIR] = total.reshape(PAIR, rows, width)


def near_kernel(shifts_ref, facts_ref, proj_ref, green_ref, total_ref):
    @pl.when(pl.program_id(0) == 0)
    def _():
        total_ref[...] = jnp.zeros_like(total_ref)

    add_products(shifts_ref, facts_ref, proj_ref, green_ref, total_ref, 0, False, 0)


def far_kernel(offset, shifts_ref, facts_ref, proj_ref, green_ref, before_ref, total_ref):
    @pl.when(pl.program_id(0) == 0)
    def _():
        total_ref[...] = before_ref[...]

    add_products(shifts_ref, facts_ref, proj_ref, green_ref, total_ref, 0, True, offset)


def last_kernel(
    start,
    offset,
    shifts_ref,
    facts_ref,
    core_ref,
    proj_ref,
    green_ref,
    before_ref,
    keep_ref,
    send_ref,
    total_ref,
):
    @pl.when(pl.program_id(0) == 0)
    def _():
        total_ref[...] = before_ref[...]

    add_products(shifts_ref, facts_ref, proj_ref, green_ref, total_ref, start, True, offset)

    @pl.when(pl.program_id(0) == pl.num_programs(0) - 1)
    def _():
        half = keep_ref.shape[1]
        core = core_ref[0]
        own = pl.multiple_of(core * half, half)
        other = pl.multiple_of((1 - core) * half, half)
        keep_ref[...] = total_ref[:, pl.ds(own, half), :]
        send_ref[...] = total_ref[:, pl.ds(other, half), :].astype(send_ref.dtype)


def products(shifts, facts, proj, green, offset=0, before=None, core=None, group=0):
    slots, rows, width = proj.shape
    energies, _, orbitals, _ = green.shape
    step = math.gcd(STEP, energies)
    photons = shifts.shape[0]
    smem = pl.BlockSpec(memory_space=pltpu.SMEM)
    if core is not None:
        photons //= GROUPS
    block = (photons, rows, width)
    operands, specs = [shifts, facts], [smem, smem]
    if core is not None:
        operands.append(core)
        specs.append(smem)
    operands += [proj, green]
    specs += [
        pl.BlockSpec((slots, rows, width), lambda t: (0, 0, 0), pipeline_mode=pl.Buffered(1)),
        pl.BlockSpec((step, 2, orbitals, orbitals), lambda t: (t, 0, 0, 0)),
    ]
    if before is not None:
        operands.append(before)
        specs.append(
            pl.BlockSpec(block, lambda t: (group, 0, 0), pipeline_mode=pl.Buffered(1))
        )
    scratch = []
    if core is not None:
        half = (photons, rows // 2, width)
        kernel = functools.partial(last_kernel, group * photons, offset)
        out_specs = [pl.BlockSpec(half, lambda t: (0, 0, 0))] * 2
        out_shape = [
            jax.ShapeDtypeStruct(half, jnp.float32),
            jax.ShapeDtypeStruct(half, jnp.bfloat16),
        ]
        scratch = [pltpu.VMEM(block, jnp.float32)]
    else:
        kernel = near_kernel if before is None else functools.partial(far_kernel, offset)
        out_specs = pl.BlockSpec(block, lambda t: (0, 0, 0))
        out_shape = jax.ShapeDtypeStruct(block, jnp.float32)
    return pl.pallas_call(
        kernel,
        out_shape=out_shape,
        grid=(energies // step,),
        in_specs=specs,
        out_specs=out_specs,
        scratch_shapes=scratch,
        compiler_params=pltpu.CompilerParams(vmem_limit_bytes=24 * MIB),
    )(*operands)


def pick(blocks, place):
    return lax.dynamic_index_in_dim(blocks, place, 0, keepdims=False)


def reduced(keep, send, planes, share):
    devices = 4 * planes
    index = lax.axis_index("energy")
    plane, chip = index // 4, (index // 2) % 2
    photons, half, width = keep.shape
    got = lax.ppermute(send, "energy", [(i, i ^ 1) for i in range(devices)])
    both = keep + got.astype(jnp.float32)
    both = both.reshape(photons, 2, planes, share, width)
    both = jnp.transpose(both, (1, 2, 0, 3, 4))
    send = pick(both, 1 - chip).astype(jnp.bfloat16)
    got = lax.ppermute(send, "energy", [(i, i ^ 2) for i in range(devices)])
    both = pick(both, chip) + got.astype(jnp.float32)
    total = pick(both, plane)
    for step in range(1, planes):
        send = pick(both, (plane + step) % planes).astype(jnp.bfloat16)
        route = [(i, (i + 4 * step) % devices) for i in range(devices)]
        total = total + lax.ppermute(send, "energy", route).astype(jnp.float32)
    return total


def on_device(lesser, greater, dipole, shifts, window):
    e_dev, _, orbitals, _ = lesser.shape
    photons = shifts.shape[0]
    devices = lax.axis_size("energy")
    index = lax.axis_index("energy")
    core = index % 2
    share = orbitals // devices
    total = e_dev * devices

    up = [(i, i + 2) for i in range(devices - 2)]
    across = [(i, i ^ 1) for i in range(devices)]
    sizes = [e_dev * part // 32 for part in PARTS]
    pieces = list(cut(greater, sizes))
    far = [lax.ppermute(pieces[0], "energy", up)]

    planes = devices // 4
    rows = dipole.reshape(2, planes, 2, 2, share, orbitals)
    rows = jnp.transpose(rows, (0, 3, 2, 1, 4, 5)).reshape(2, orbitals, orbitals)
    left = jnp.concatenate([rows[0], rows[1]], 1)
    real, imag = dipole[0].T, dipole[1].T
    right = jnp.concatenate(
        [jnp.concatenate([real, -imag], 1), jnp.concatenate([imag, real], 1)], 0
    )
    proj = project(left, right, lesser, lax.ppermute(lesser, "energy", across))

    pieces[1], proj = lax.optimization_barrier((pieces[1], proj))
    far.append(lax.ppermute(pieces[1], "energy", up))

    limit = jnp.where(core == 0, 2 * e_dev, e_dev)
    facts = jnp.stack([window[0], window[1], index * e_dev, limit, jnp.int32(e_dev)])
    facts = facts.astype(jnp.int32)
    result = products(shifts, facts, proj, greater)
    pieces[2], result = lax.optimization_barrier((pieces[2], result))
    far.append(lax.ppermute(pieces[2], "energy", up))
    core = core[None]
    first = 0
    for block, size in zip(far[:-1], sizes):
        result = products(shifts, facts, proj, block, offset=first, before=result)
        first += size
    sums = []
    for group in range(GROUPS):
        keep, send = products(
            shifts, facts, proj, far[-1], offset=first, before=result, core=core, group=group
        )
        sums.append(reduced(keep, send, planes, share))
    scale = 1.0 / math.sqrt(2.0 * orbitals * total)
    summed = jnp.concatenate(sums, 0) * scale
    summed = jnp.transpose(summed, (1, 0, 2))
    return summed.reshape(share, photons, 2, orbitals)


def solution(mesh):
    placed = (
        P(("dom", "energy"), None, None, None),
        P(("dom", "energy"), None, None, None),
        P(),
        P(),
        P("dom"),
    )
    return jax.shard_map(
        on_device,
        mesh=mesh,
        in_specs=placed,
        out_specs=P(("dom", "energy"), None, None, None),
        check_vma=False,
    )
```

```python
import functools
import math

import jax
import jax.numpy as jnp
from jax import lax
from jax.experimental import pallas as pl
from jax.experimental.pallas import tpu as pltpu
from jax.sharding import PartitionSpec as P

STEP = 8
WIDE = 16
PAIR = 2
GROUPS = 1
PARTS = (16, 8, 6, 2)
MIB = 1 << 20


def rotated(real, imag):
    top = jnp.concatenate([real, imag], 1)
    bottom = jnp.concatenate([-imag, real], 1)
    return jnp.concatenate([top, bottom], 0)


def cut_kernel(first, sizes, source_ref, *refs):
    sems = refs[-1]
    copies = []
    for k, size in enumerate(sizes):
        copies.append(
            pltpu.make_async_copy(source_ref.at[pl.ds(first, size)], refs[k], sems.at[k])
        )
        copies[-1].start()
        first += size
    for copy in copies:
        copy.wait()


def cut(blocks, first, sizes, limit):
    return pl.pallas_call(
        functools.partial(cut_kernel, first, sizes),
        out_shape=[pltpu.VMEM((size,) + blocks.shape[1:], blocks.dtype) for size in sizes],
        in_specs=[pl.BlockSpec(memory_space=pl.ANY)],
        out_specs=[pl.BlockSpec(memory_space=pltpu.VMEM)] * len(sizes),
        scratch_shapes=[pltpu.SemaphoreType.DMA((len(sizes),))],
        compiler_params=pltpu.CompilerParams(vmem_limit_bytes=limit * MIB),
    )(blocks)


def project_blocks(left, right, lesser_ref, out_ref):
    count, rows, width = out_ref.shape
    inner = [
        jnp.dot(
            left,
            rotated(lesser_ref[u, 0], lesser_ref[u, 1]),
            preferred_element_type=jnp.float32,
        )
        for u in range(count)
    ]
    inner = jnp.concatenate(inner, 0)
    high = inner.astype(jnp.bfloat16)
    low = (inner - high.astype(jnp.float32)).astype(jnp.bfloat16)
    outer = jnp.dot(high, right, preferred_element_type=jnp.float32)
    outer += jnp.dot(low, right, preferred_element_type=jnp.float32)
    out_ref[...] = outer.astype(jnp.bfloat16).reshape(count, rows, width)


def project_kernel(steps, left_ref, right_ref, own_ref, other_ref, out_ref):
    t = pl.program_id(0)

    @pl.when(t < steps)
    def _():
        project_blocks(left_ref[...], right_ref[...], own_ref, out_ref)

    @pl.when((t >= steps) & (t < 2 * steps))
    def _():
        project_blocks(left_ref[...], right_ref[...], other_ref, out_ref)

    @pl.when(t == 2 * steps)
    def _():
        out_ref[...] = jnp.zeros_like(out_ref)


def project(left, right, own, other):
    energies, _, orbitals, _ = own.shape
    width = 2 * orbitals
    steps = energies // WIDE
    slots = 2 * energies + WIDE
    return pl.pallas_call(
        functools.partial(project_kernel, steps),
        out_shape=jax.ShapeDtypeStruct((slots, orbitals, width), jnp.bfloat16),
        grid=(2 * steps + 1,),
        in_specs=[
            pl.BlockSpec((orbitals, width), lambda t: (0, 0)),
            pl.BlockSpec((width, width), lambda t: (0, 0)),
            pl.BlockSpec(
                (WIDE, 2, orbitals, orbitals), lambda t: (jnp.minimum(t, steps - 1), 0, 0, 0)
            ),
            pl.BlockSpec(
                (WIDE, 2, orbitals, orbitals),
                lambda t: (jnp.clip(t - steps, 0, steps - 1), 0, 0, 0),
            ),
        ],
        out_specs=pl.BlockSpec((WIDE, orbitals, width), lambda t: (t, 0, 0)),
        compiler_params=pltpu.CompilerParams(vmem_limit_bytes=16 * MIB),
    )(left, right, own, other)


def pair_place(shift, offset, far, facts_ref, zero_place):
    low, high, base, limit, e_dev = (facts_ref[i] for i in range(5))
    reach = offset + shift
    energy = base + offset
    if far:
        energy = energy - 2 * e_dev
    met = reach >= limit if far else reach < limit
    met = met & (energy >= low) & (energy + shift < high)
    if far:
        reach = jnp.where(reach >= 2 * e_dev, reach - 2 * e_dev, reach)
    return jnp.where(met, reach, zero_place)


def add_products(shifts_ref, facts_ref, proj_ref, green_ref, total_ref, start, far, offset):
    step = green_ref.shape[0]
    first = pl.program_id(0) * step + offset
    photons, rows, width = total_ref.shape
    zero_place = proj_ref.shape[0] - 1
    for w in range(0, photons, PAIR):
        shifts = [shifts_ref[start + w + v] for v in range(PAIR)]
        total = total_ref[w : w + PAIR].reshape(PAIR * rows, width)
        for u in range(step):
            places = [pair_place(shift, first + u, far, facts_ref, zero_place) for shift in shifts]
            left = jnp.concatenate([proj_ref[place] for place in places], 0)
            right = rotated(green_ref[u, 0], green_ref[u, 1])
            total += jnp.dot(left, right, preferred_element_type=jnp.float32)
        total_ref[w : w + PAIR] = total.reshape(PAIR, rows, width)


def near_kernel(shifts_ref, facts_ref, proj_ref, green_ref, total_ref):
    @pl.when(pl.program_id(0) == 0)
    def _():
        total_ref[...] = jnp.zeros_like(total_ref)

    add_products(shifts_ref, facts_ref, proj_ref, green_ref, total_ref, 0, False, 0)


def far_kernel(offset, shifts_ref, facts_ref, proj_ref, green_ref, before_ref, total_ref):
    @pl.when(pl.program_id(0) == 0)
    def _():
        total_ref[...] = before_ref[...]

    add_products(shifts_ref, facts_ref, proj_ref, green_ref, total_ref, 0, True, offset)


def last_kernel(
    start,
    offset,
    shifts_ref,
    facts_ref,
    core_ref,
    proj_ref,
    green_ref,
    before_ref,
    keep_ref,
    send_ref,
    total_ref,
):
    @pl.when(pl.program_id(0) == 0)
    def _():
        total_ref[...] = before_ref[...]

    add_products(shifts_ref, facts_ref, proj_ref, green_ref, total_ref, start, True, offset)

    @pl.when(pl.program_id(0) == pl.num_programs(0) - 1)
    def _():
        half = keep_ref.shape[1]
        core = core_ref[0]
        own = pl.multiple_of(core * half, half)
        other = pl.multiple_of((1 - core) * half, half)
        keep_ref[...] = total_ref[:, pl.ds(own, half), :]
        send_ref[...] = total_ref[:, pl.ds(other, half), :].astype(send_ref.dtype)


def products(shifts, facts, proj, green, offset=0, before=None, core=None, group=0):
    slots, rows, width = proj.shape
    energies, _, orbitals, _ = green.shape
    step = math.gcd(STEP, energies)
    photons = shifts.shape[0]
    smem = pl.BlockSpec(memory_space=pltpu.SMEM)
    if core is not None:
        photons //= GROUPS
    block = (photons, rows, width)
    operands, specs = [shifts, facts], [smem, smem]
    if core is not None:
        operands.append(core)
        specs.append(smem)
    operands += [proj, green]
    specs += [
        pl.BlockSpec((slots, rows, width), lambda t: (0, 0, 0), pipeline_mode=pl.Buffered(1)),
        pl.BlockSpec((step, 2, orbitals, orbitals), lambda t: (t, 0, 0, 0)),
    ]
    if before is not None:
        operands.append(before)
        specs.append(
            pl.BlockSpec(block, lambda t: (group, 0, 0), pipeline_mode=pl.Buffered(1))
        )
    scratch = []
    if core is not None:
        half = (photons, rows // 2, width)
        kernel = functools.partial(last_kernel, group * photons, offset)
        out_specs = [pl.BlockSpec(half, lambda t: (0, 0, 0))] * 2
        out_shape = [
            jax.ShapeDtypeStruct(half, jnp.float32),
            jax.ShapeDtypeStruct(half, jnp.bfloat16),
        ]
        scratch = [pltpu.VMEM(block, jnp.float32)]
    else:
        kernel = near_kernel if before is None else functools.partial(far_kernel, offset)
        out_specs = pl.BlockSpec(block, lambda t: (0, 0, 0))
        out_shape = jax.ShapeDtypeStruct(block, jnp.float32)
    return pl.pallas_call(
        kernel,
        out_shape=out_shape,
        grid=(energies // step,),
        in_specs=specs,
        out_specs=out_specs,
        scratch_shapes=scratch,
        compiler_params=pltpu.CompilerParams(vmem_limit_bytes=24 * MIB),
    )(*operands)


def pick(blocks, place):
    return lax.dynamic_index_in_dim(blocks, place, 0, keepdims=False)


def reduced(keep, send, planes, share):
    devices = 4 * planes
    index = lax.axis_index("energy")
    plane, chip = index // 4, (index // 2) % 2
    photons, half, width = keep.shape
    got = lax.ppermute(send, "energy", [(i, i ^ 1) for i in range(devices)])
    both = keep + got.astype(jnp.float32)
    both = both.reshape(photons, 2, planes, share, width)
    both = jnp.transpose(both, (1, 2, 0, 3, 4))
    send = pick(both, 1 - chip).astype(jnp.bfloat16)
    got = lax.ppermute(send, "energy", [(i, i ^ 2) for i in range(devices)])
    both = pick(both, chip) + got.astype(jnp.float32)
    total = pick(both, plane)
    for step in range(1, planes):
        send = pick(both, (plane + step) % planes).astype(jnp.bfloat16)
        route = [(i, (i + 4 * step) % devices) for i in range(devices)]
        total = total + lax.ppermute(send, "energy", route).astype(jnp.float32)
    return total


def on_device(lesser, greater, dipole, shifts, window):
    e_dev, _, orbitals, _ = lesser.shape
    photons = shifts.shape[0]
    devices = lax.axis_size("energy")
    index = lax.axis_index("energy")
    core = index % 2
    share = orbitals // devices
    total = e_dev * devices

    up = [(i, i + 2) for i in range(devices - 2)]
    across = [(i, i ^ 1) for i in range(devices)]
    sizes = [e_dev * part // 32 for part in PARTS]
    pieces = list(cut(greater, 0, sizes[:1], 50))
    far = [lax.ppermute(pieces[0], "energy", up)]

    planes = devices // 4
    rows = dipole.reshape(2, planes, 2, 2, share, orbitals)
    rows = jnp.transpose(rows, (0, 3, 2, 1, 4, 5)).reshape(2, orbitals, orbitals)
    left = jnp.concatenate([rows[0], rows[1]], 1)
    real, imag = dipole[0].T, dipole[1].T
    right = jnp.concatenate(
        [jnp.concatenate([real, -imag], 1), jnp.concatenate([imag, real], 1)], 0
    )
    proj = project(left, right, lesser, lax.ppermute(lesser, "energy", across))

    rest, proj = lax.optimization_barrier((greater, proj))
    pieces += list(cut(rest, sizes[0], sizes[1:], 8))
    far.append(lax.ppermute(pieces[1], "energy", up))

    limit = jnp.where(core == 0, 2 * e_dev, e_dev)
    facts = jnp.stack([window[0], window[1], index * e_dev, limit, jnp.int32(e_dev)])
    facts = facts.astype(jnp.int32)
    result = products(shifts, facts, proj, greater)
    core = core[None]
    first = 0
    for k, size in enumerate(sizes[:-1]):
        if k + 2 < len(sizes):
            pieces[k + 2], result = lax.optimization_barrier((pieces[k + 2], result))
            far.append(lax.ppermute(pieces[k + 2], "energy", up))
        result = products(shifts, facts, proj, far[k], offset=first, before=result)
        first += size
    sums = []
    for group in range(GROUPS):
        keep, send = products(
            shifts, facts, proj, far[-1], offset=first, before=result, core=core, group=group
        )
        sums.append(reduced(keep, send, planes, share))
    scale = 1.0 / math.sqrt(2.0 * orbitals * total)
    summed = jnp.concatenate(sums, 0) * scale
    summed = jnp.transpose(summed, (1, 0, 2))
    return summed.reshape(share, photons, 2, orbitals)


def solution(mesh):
    placed = (
        P(("dom", "energy"), None, None, None),
        P(("dom", "energy"), None, None, None),
        P(),
        P(),
        P("dom"),
    )
    return jax.shard_map(
        on_device,
        mesh=mesh,
        in_specs=placed,
        out_specs=P(("dom", "energy"), None, None, None),
        check_vma=False,
    )
```

```python
import functools
import math

import jax
import jax.numpy as jnp
from jax import lax
from jax.experimental import pallas as pl
from jax.experimental.pallas import tpu as pltpu
from jax.sharding import PartitionSpec as P

STEP = 8
WIDE = 16
PAIR = 2
GROUPS = 1
PARTS = (16, 8, 6, 2)
MIB = 1 << 20


def rotated(real, imag):
    top = jnp.concatenate([real, imag], 1)
    bottom = jnp.concatenate([-imag, real], 1)
    return jnp.concatenate([top, bottom], 0)


def cut_kernel(first, sizes, source_ref, *refs):
    sems = refs[-1]
    copies = []
    for k, size in enumerate(sizes):
        copies.append(
            pltpu.make_async_copy(source_ref.at[pl.ds(first, size)], refs[k], sems.at[k])
        )
        copies[-1].start()
        first += size
    for copy in copies:
        copy.wait()


def cut(blocks, first, sizes, limit):
    return pl.pallas_call(
        functools.partial(cut_kernel, first, sizes),
        out_shape=[pltpu.VMEM((size,) + blocks.shape[1:], blocks.dtype) for size in sizes],
        in_specs=[pl.BlockSpec(memory_space=pl.ANY)],
        out_specs=[pl.BlockSpec(memory_space=pltpu.VMEM)] * len(sizes),
        scratch_shapes=[pltpu.SemaphoreType.DMA((len(sizes),))],
        compiler_params=pltpu.CompilerParams(vmem_limit_bytes=limit * MIB),
    )(blocks)


def project_blocks(left, right, lesser_ref, out_ref):
    count, rows, width = out_ref.shape
    inner = [
        jnp.dot(
            left,
            rotated(lesser_ref[u, 0], lesser_ref[u, 1]),
            preferred_element_type=jnp.float32,
        )
        for u in range(count)
    ]
    inner = jnp.concatenate(inner, 0)
    high = inner.astype(jnp.bfloat16)
    low = (inner - high.astype(jnp.float32)).astype(jnp.bfloat16)
    outer = jnp.dot(high, right, preferred_element_type=jnp.float32)
    outer += jnp.dot(low, right, preferred_element_type=jnp.float32)
    out_ref[...] = outer.astype(jnp.bfloat16).reshape(count, rows, width)


def project_kernel(steps, left_ref, right_ref, own_ref, other_ref, out_ref):
    t = pl.program_id(0)

    @pl.when(t < steps)
    def _():
        project_blocks(left_ref[...], right_ref[...], own_ref, out_ref)

    @pl.when((t >= steps) & (t < 2 * steps))
    def _():
        project_blocks(left_ref[...], right_ref[...], other_ref, out_ref)

    @pl.when(t == 2 * steps)
    def _():
        out_ref[...] = jnp.zeros_like(out_ref)


def project(left, right, own, other):
    energies, _, orbitals, _ = own.shape
    width = 2 * orbitals
    steps = energies // WIDE
    slots = 2 * energies + WIDE
    return pl.pallas_call(
        functools.partial(project_kernel, steps),
        out_shape=jax.ShapeDtypeStruct((slots, orbitals, width), jnp.bfloat16),
        grid=(2 * steps + 1,),
        in_specs=[
            pl.BlockSpec((orbitals, width), lambda t: (0, 0)),
            pl.BlockSpec((width, width), lambda t: (0, 0)),
            pl.BlockSpec(
                (WIDE, 2, orbitals, orbitals), lambda t: (jnp.minimum(t, steps - 1), 0, 0, 0)
            ),
            pl.BlockSpec(
                (WIDE, 2, orbitals, orbitals),
                lambda t: (jnp.clip(t - steps, 0, steps - 1), 0, 0, 0),
            ),
        ],
        out_specs=pl.BlockSpec((WIDE, orbitals, width), lambda t: (t, 0, 0)),
        compiler_params=pltpu.CompilerParams(vmem_limit_bytes=16 * MIB),
    )(left, right, own, other)


def pair_place(shift, offset, far, facts_ref, zero_place):
    low, high, base, limit, e_dev = (facts_ref[i] for i in range(5))
    reach = offset + shift
    energy = base + offset
    if far:
        energy = energy - 2 * e_dev
    met = reach >= limit if far else reach < limit
    met = met & (energy >= low) & (energy + shift < high)
    if far:
        reach = jnp.where(reach >= 2 * e_dev, reach - 2 * e_dev, reach)
    return jnp.where(met, reach, zero_place)


def add_products(shifts_ref, facts_ref, proj_ref, green_ref, total_ref, start, far, offset):
    step = green_ref.shape[0]
    first = pl.program_id(0) * step + offset
    photons, rows, width = total_ref.shape
    zero_place = proj_ref.shape[0] - 1
    for w in range(0, photons, PAIR):
        shifts = [shifts_ref[start + w + v] for v in range(PAIR)]
        total = total_ref[w : w + PAIR].reshape(PAIR * rows, width)
        for u in range(step):
            places = [pair_place(shift, first + u, far, facts_ref, zero_place) for shift in shifts]
            left = jnp.concatenate([proj_ref[place] for place in places], 0)
            right = rotated(green_ref[u, 0], green_ref[u, 1])
            total += jnp.dot(left, right, preferred_element_type=jnp.float32)
        total_ref[w : w + PAIR] = total.reshape(PAIR, rows, width)


def near_kernel(shifts_ref, facts_ref, proj_ref, green_ref, total_ref):
    @pl.when(pl.program_id(0) == 0)
    def _():
        total_ref[...] = jnp.zeros_like(total_ref)

    add_products(shifts_ref, facts_ref, proj_ref, green_ref, total_ref, 0, False, 0)


def far_kernel(offset, shifts_ref, facts_ref, proj_ref, green_ref, before_ref, total_ref):
    @pl.when(pl.program_id(0) == 0)
    def _():
        total_ref[...] = before_ref[...]

    add_products(shifts_ref, facts_ref, proj_ref, green_ref, total_ref, 0, True, offset)


def last_kernel(
    start,
    offset,
    shifts_ref,
    facts_ref,
    core_ref,
    proj_ref,
    green_ref,
    before_ref,
    keep_ref,
    send_ref,
    total_ref,
):
    @pl.when(pl.program_id(0) == 0)
    def _():
        total_ref[...] = before_ref[...]

    add_products(shifts_ref, facts_ref, proj_ref, green_ref, total_ref, start, True, offset)

    @pl.when(pl.program_id(0) == pl.num_programs(0) - 1)
    def _():
        half = keep_ref.shape[1]
        core = core_ref[0]
        own = pl.multiple_of(core * half, half)
        other = pl.multiple_of((1 - core) * half, half)
        keep_ref[...] = total_ref[:, pl.ds(own, half), :]
        send_ref[...] = total_ref[:, pl.ds(other, half), :].astype(send_ref.dtype)


def products(shifts, facts, proj, green, offset=0, before=None, core=None, group=0):
    slots, rows, width = proj.shape
    energies, _, orbitals, _ = green.shape
    step = math.gcd(STEP, energies)
    photons = shifts.shape[0]
    smem = pl.BlockSpec(memory_space=pltpu.SMEM)
    if core is not None:
        photons //= GROUPS
    block = (photons, rows, width)
    operands, specs = [shifts, facts], [smem, smem]
    if core is not None:
        operands.append(core)
        specs.append(smem)
    operands += [proj, green]
    specs += [
        pl.BlockSpec((slots, rows, width), lambda t: (0, 0, 0), pipeline_mode=pl.Buffered(1)),
        pl.BlockSpec((step, 2, orbitals, orbitals), lambda t: (t, 0, 0, 0)),
    ]
    if before is not None:
        operands.append(before)
        specs.append(
            pl.BlockSpec(block, lambda t: (group, 0, 0), pipeline_mode=pl.Buffered(1))
        )
    scratch = []
    if core is not None:
        half = (photons, rows // 2, width)
        kernel = functools.partial(last_kernel, group * photons, offset)
        out_specs = [pl.BlockSpec(half, lambda t: (0, 0, 0))] * 2
        out_shape = [
            jax.ShapeDtypeStruct(half, jnp.float32),
            jax.ShapeDtypeStruct(half, jnp.bfloat16),
        ]
        scratch = [pltpu.VMEM(block, jnp.float32)]
    else:
        kernel = near_kernel if before is None else functools.partial(far_kernel, offset)
        out_specs = pl.BlockSpec(block, lambda t: (0, 0, 0))
        out_shape = jax.ShapeDtypeStruct(block, jnp.float32)
    return pl.pallas_call(
        kernel,
        out_shape=out_shape,
        grid=(energies // step,),
        in_specs=specs,
        out_specs=out_specs,
        scratch_shapes=scratch,
        compiler_params=pltpu.CompilerParams(vmem_limit_bytes=24 * MIB),
    )(*operands)


def pick(blocks, place):
    return lax.dynamic_index_in_dim(blocks, place, 0, keepdims=False)


def reduced(keep, send, planes, share):
    devices = 4 * planes
    index = lax.axis_index("energy")
    plane, chip = index // 4, (index // 2) % 2
    photons, half, width = keep.shape
    got = lax.ppermute(send, "energy", [(i, i ^ 1) for i in range(devices)])
    both = keep + got.astype(jnp.float32)
    both = both.reshape(photons, 2, planes, share, width)
    both = jnp.transpose(both, (1, 2, 0, 3, 4))
    theirs, mine = pick(both, 1 - chip), pick(both, chip)
    steps = sorted(range(1, planes), key=lambda k: -min(k, planes - k)) + [0]
    sums = []
    for part in (steps[: planes // 2], steps[planes // 2 :]):
        at = [(plane + step) % planes for step in part]
        send = jnp.stack([pick(theirs, k) for k in at]).astype(jnp.bfloat16)
        got = lax.ppermute(send, "energy", [(i, i ^ 2) for i in range(devices)])
        sums += [pick(mine, k) + got[n].astype(jnp.float32) for n, k in enumerate(at)]
        mine = lax.optimization_barrier(mine)
    total = sums[-1]
    for step, block in zip(steps[:-1], sums):
        route = [(i, (i + 4 * step) % devices) for i in range(devices)]
        total = total + lax.ppermute(block.astype(jnp.bfloat16), "energy", route).astype(
            jnp.float32
        )
    return total


def on_device(lesser, greater, dipole, shifts, window):
    e_dev, _, orbitals, _ = lesser.shape
    photons = shifts.shape[0]
    devices = lax.axis_size("energy")
    index = lax.axis_index("energy")
    core = index % 2
    share = orbitals // devices
    total = e_dev * devices

    up = [(i, i + 2) for i in range(devices - 2)]
    across = [(i, i ^ 1) for i in range(devices)]
    sizes = [e_dev * part // 32 for part in PARTS]
    pieces = list(cut(greater, 0, sizes[:1], 50))
    far = [lax.ppermute(pieces[0], "energy", up)]

    planes = devices // 4
    rows = dipole.reshape(2, planes, 2, 2, share, orbitals)
    rows = jnp.transpose(rows, (0, 3, 2, 1, 4, 5)).reshape(2, orbitals, orbitals)
    left = jnp.concatenate([rows[0], rows[1]], 1)
    real, imag = dipole[0].T, dipole[1].T
    right = jnp.concatenate(
        [jnp.concatenate([real, -imag], 1), jnp.concatenate([imag, real], 1)], 0
    )
    proj = project(left, right, lesser, lax.ppermute(lesser, "energy", across))

    rest, proj = lax.optimization_barrier((greater, proj))
    pieces += list(cut(rest, sizes[0], sizes[1:], 8))
    far.append(lax.ppermute(pieces[1], "energy", up))

    limit = jnp.where(core == 0, 2 * e_dev, e_dev)
    facts = jnp.stack([window[0], window[1], index * e_dev, limit, jnp.int32(e_dev)])
    facts = facts.astype(jnp.int32)
    result = products(shifts, facts, proj, greater)
    core = core[None]
    first = 0
    for k, size in enumerate(sizes[:-1]):
        if k + 2 < len(sizes):
            pieces[k + 2], result = lax.optimization_barrier((pieces[k + 2], result))
            far.append(lax.ppermute(pieces[k + 2], "energy", up))
        result = products(shifts, facts, proj, far[k], offset=first, before=result)
        first += size
    sums = []
    for group in range(GROUPS):
        keep, send = products(
            shifts, facts, proj, far[-1], offset=first, before=result, core=core, group=group
        )
        sums.append(reduced(keep, send, planes, share))
    scale = 1.0 / math.sqrt(2.0 * orbitals * total)
    summed = jnp.concatenate(sums, 0) * scale
    summed = jnp.transpose(summed, (1, 0, 2))
    return summed.reshape(share, photons, 2, orbitals)


def solution(mesh):
    placed = (
        P(("dom", "energy"), None, None, None),
        P(("dom", "energy"), None, None, None),
        P(),
        P(),
        P("dom"),
    )
    return jax.shard_map(
        on_device,
        mesh=mesh,
        in_specs=placed,
        out_specs=P(("dom", "energy"), None, None, None),
        check_vma=False,
    )
```

```python
import functools
import math

import jax
import jax.numpy as jnp
from jax import lax
from jax.experimental import pallas as pl
from jax.experimental.pallas import tpu as pltpu
from jax.sharding import PartitionSpec as P

STEP = 8
WIDE = 16
PAIR = 2
GROUPS = 1
PARTS = (20, 6, 4, 2)
MIB = 1 << 20


def rotated(real, imag):
    top = jnp.concatenate([real, imag], 1)
    bottom = jnp.concatenate([-imag, real], 1)
    return jnp.concatenate([top, bottom], 0)


def cut_kernel(first, sizes, source_ref, *refs):
    sems = refs[-1]
    copies = []
    for k, size in enumerate(sizes):
        copies.append(
            pltpu.make_async_copy(source_ref.at[pl.ds(first, size)], refs[k], sems.at[k])
        )
        copies[-1].start()
        first += size
    for copy in copies:
        copy.wait()


def cut(blocks, first, sizes, limit):
    return pl.pallas_call(
        functools.partial(cut_kernel, first, sizes),
        out_shape=[pltpu.VMEM((size,) + blocks.shape[1:], blocks.dtype) for size in sizes],
        in_specs=[pl.BlockSpec(memory_space=pl.ANY)],
        out_specs=[pl.BlockSpec(memory_space=pltpu.VMEM)] * len(sizes),
        scratch_shapes=[pltpu.SemaphoreType.DMA((len(sizes),))],
        compiler_params=pltpu.CompilerParams(vmem_limit_bytes=limit * MIB),
    )(blocks)


def project_blocks(left, right, lesser_ref, out_ref):
    count, rows, width = out_ref.shape
    inner = [
        jnp.dot(
            left,
            rotated(lesser_ref[u, 0], lesser_ref[u, 1]),
            preferred_element_type=jnp.float32,
        )
        for u in range(count)
    ]
    inner = jnp.concatenate(inner, 0)
    high = inner.astype(jnp.bfloat16)
    low = (inner - high.astype(jnp.float32)).astype(jnp.bfloat16)
    outer = jnp.dot(high, right, preferred_element_type=jnp.float32)
    outer += jnp.dot(low, right, preferred_element_type=jnp.float32)
    out_ref[...] = outer.astype(jnp.bfloat16).reshape(count, rows, width)


def project_kernel(steps, left_ref, right_ref, own_ref, other_ref, out_ref):
    t = pl.program_id(0)

    @pl.when(t < steps)
    def _():
        project_blocks(left_ref[...], right_ref[...], own_ref, out_ref)

    @pl.when((t >= steps) & (t < 2 * steps))
    def _():
        project_blocks(left_ref[...], right_ref[...], other_ref, out_ref)

    @pl.when(t == 2 * steps)
    def _():
        out_ref[...] = jnp.zeros_like(out_ref)


def project(left, right, own, other):
    energies, _, orbitals, _ = own.shape
    width = 2 * orbitals
    steps = energies // WIDE
    slots = 2 * energies + WIDE
    return pl.pallas_call(
        functools.partial(project_kernel, steps),
        out_shape=jax.ShapeDtypeStruct((slots, orbitals, width), jnp.bfloat16),
        grid=(2 * steps + 1,),
        in_specs=[
            pl.BlockSpec((orbitals, width), lambda t: (0, 0)),
            pl.BlockSpec((width, width), lambda t: (0, 0)),
            pl.BlockSpec(
                (WIDE, 2, orbitals, orbitals), lambda t: (jnp.minimum(t, steps - 1), 0, 0, 0)
            ),
            pl.BlockSpec(
                (WIDE, 2, orbitals, orbitals),
                lambda t: (jnp.clip(t - steps, 0, steps - 1), 0, 0, 0),
            ),
        ],
        out_specs=pl.BlockSpec((WIDE, orbitals, width), lambda t: (t, 0, 0)),
        compiler_params=pltpu.CompilerParams(vmem_limit_bytes=16 * MIB),
    )(left, right, own, other)


def pair_place(shift, offset, far, facts_ref, zero_place):
    low, high, base, limit, e_dev = (facts_ref[i] for i in range(5))
    reach = offset + shift
    energy = base + offset
    if far:
        energy = energy - 2 * e_dev
    met = reach >= limit if far else reach < limit
    met = met & (energy >= low) & (energy + shift < high)
    if far:
        reach = jnp.where(reach >= 2 * e_dev, reach - 2 * e_dev, reach)
    return jnp.where(met, reach, zero_place)


def add_products(shifts_ref, facts_ref, proj_ref, green_ref, total_ref, start, far, offset):
    step = green_ref.shape[0]
    first = pl.program_id(0) * step + offset
    photons, rows, width = total_ref.shape
    zero_place = proj_ref.shape[0] - 1
    for w in range(0, photons, PAIR):
        shifts = [shifts_ref[start + w + v] for v in range(PAIR)]
        total = total_ref[w : w + PAIR].reshape(PAIR * rows, width)
        for u in range(step):
            places = [pair_place(shift, first + u, far, facts_ref, zero_place) for shift in shifts]
            left = jnp.concatenate([proj_ref[place] for place in places], 0)
            right = rotated(green_ref[u, 0], green_ref[u, 1])
            total += jnp.dot(left, right, preferred_element_type=jnp.float32)
        total_ref[w : w + PAIR] = total.reshape(PAIR, rows, width)


def near_kernel(shifts_ref, facts_ref, proj_ref, green_ref, total_ref):
    @pl.when(pl.program_id(0) == 0)
    def _():
        total_ref[...] = jnp.zeros_like(total_ref)

    add_products(shifts_ref, facts_ref, proj_ref, green_ref, total_ref, 0, False, 0)


def far_kernel(offset, shifts_ref, facts_ref, proj_ref, green_ref, before_ref, total_ref):
    @pl.when(pl.program_id(0) == 0)
    def _():
        total_ref[...] = before_ref[...]

    add_products(shifts_ref, facts_ref, proj_ref, green_ref, total_ref, 0, True, offset)


def last_kernel(
    start,
    offset,
    shifts_ref,
    facts_ref,
    core_ref,
    proj_ref,
    green_ref,
    before_ref,
    keep_ref,
    send_ref,
    total_ref,
):
    @pl.when(pl.program_id(0) == 0)
    def _():
        total_ref[...] = before_ref[...]

    add_products(shifts_ref, facts_ref, proj_ref, green_ref, total_ref, start, True, offset)

    @pl.when(pl.program_id(0) == pl.num_programs(0) - 1)
    def _():
        half = keep_ref.shape[1]
        core = core_ref[0]
        own = pl.multiple_of(core * half, half)
        other = pl.multiple_of((1 - core) * half, half)
        keep_ref[...] = total_ref[:, pl.ds(own, half), :]
        send_ref[...] = total_ref[:, pl.ds(other, half), :].astype(send_ref.dtype)


def products(shifts, facts, proj, green, offset=0, before=None, core=None, group=0):
    slots, rows, width = proj.shape
    energies, _, orbitals, _ = green.shape
    step = math.gcd(STEP, energies)
    photons = shifts.shape[0]
    smem = pl.BlockSpec(memory_space=pltpu.SMEM)
    if core is not None:
        photons //= GROUPS
    block = (photons, rows, width)
    operands, specs = [shifts, facts], [smem, smem]
    if core is not None:
        operands.append(core)
        specs.append(smem)
    operands += [proj, green]
    specs += [
        pl.BlockSpec((slots, rows, width), lambda t: (0, 0, 0), pipeline_mode=pl.Buffered(1)),
        pl.BlockSpec((step, 2, orbitals, orbitals), lambda t: (t, 0, 0, 0)),
    ]
    if before is not None:
        operands.append(before)
        specs.append(
            pl.BlockSpec(block, lambda t: (group, 0, 0), pipeline_mode=pl.Buffered(1))
        )
    scratch = []
    if core is not None:
        half = (photons, rows // 2, width)
        kernel = functools.partial(last_kernel, group * photons, offset)
        out_specs = [pl.BlockSpec(half, lambda t: (0, 0, 0))] * 2
        out_shape = [
            jax.ShapeDtypeStruct(half, jnp.float32),
            jax.ShapeDtypeStruct(half, jnp.bfloat16),
        ]
        scratch = [pltpu.VMEM(block, jnp.float32)]
    else:
        kernel = near_kernel if before is None else functools.partial(far_kernel, offset)
        out_specs = pl.BlockSpec(block, lambda t: (0, 0, 0))
        out_shape = jax.ShapeDtypeStruct(block, jnp.float32)
    return pl.pallas_call(
        kernel,
        out_shape=out_shape,
        grid=(energies // step,),
        in_specs=specs,
        out_specs=out_specs,
        scratch_shapes=scratch,
        compiler_params=pltpu.CompilerParams(vmem_limit_bytes=24 * MIB),
    )(*operands)


def pick(blocks, place):
    return lax.dynamic_index_in_dim(blocks, place, 0, keepdims=False)


def reduced(keep, send, planes, share):
    devices = 4 * planes
    index = lax.axis_index("energy")
    plane, chip = index // 4, (index // 2) % 2
    photons, half, width = keep.shape
    got = lax.ppermute(send, "energy", [(i, i ^ 1) for i in range(devices)])
    both = keep + got.astype(jnp.float32)
    both = both.reshape(photons, 2, planes, share, width)
    both = jnp.transpose(both, (1, 2, 0, 3, 4))
    theirs, mine = pick(both, 1 - chip), pick(both, chip)
    steps = sorted(range(1, planes), key=lambda k: -min(k, planes - k)) + [0]
    sums = []
    for part in (steps[: planes // 2], steps[planes // 2 :]):
        at = [(plane + step) % planes for step in part]
        send = jnp.stack([pick(theirs, k) for k in at]).astype(jnp.bfloat16)
        got = lax.ppermute(send, "energy", [(i, i ^ 2) for i in range(devices)])
        sums += [pick(mine, k) + got[n].astype(jnp.float32) for n, k in enumerate(at)]
        mine = lax.optimization_barrier(mine)
    total = sums[-1]
    for step, block in zip(steps[:-1], sums):
        route = [(i, (i + 4 * step) % devices) for i in range(devices)]
        total = total + lax.ppermute(block.astype(jnp.bfloat16), "energy", route).astype(
            jnp.float32
        )
    return total


def on_device(lesser, greater, dipole, shifts, window):
    e_dev, _, orbitals, _ = lesser.shape
    photons = shifts.shape[0]
    devices = lax.axis_size("energy")
    index = lax.axis_index("energy")
    core = index % 2
    share = orbitals // devices
    total = e_dev * devices

    up = [(i, i + 2) for i in range(devices - 2)]
    across = [(i, i ^ 1) for i in range(devices)]
    sizes = [e_dev * part // 32 for part in PARTS]
    pieces = list(cut(greater, 0, sizes[:1], 50))
    far = [lax.ppermute(pieces[0], "energy", up)]

    planes = devices // 4
    rows = dipole.reshape(2, planes, 2, 2, share, orbitals)
    rows = jnp.transpose(rows, (0, 3, 2, 1, 4, 5)).reshape(2, orbitals, orbitals)
    left = jnp.concatenate([rows[0], rows[1]], 1)
    real, imag = dipole[0].T, dipole[1].T
    right = jnp.concatenate(
        [jnp.concatenate([real, -imag], 1), jnp.concatenate([imag, real], 1)], 0
    )
    proj = project(left, right, lesser, lax.ppermute(lesser, "energy", across))

    rest, proj = lax.optimization_barrier((greater, proj))
    pieces += list(cut(rest, sizes[0], sizes[1:], 8))
    far.append(lax.ppermute(pieces[1], "energy", up))

    limit = jnp.where(core == 0, 2 * e_dev, e_dev)
    facts = jnp.stack([window[0], window[1], index * e_dev, limit, jnp.int32(e_dev)])
    facts = facts.astype(jnp.int32)
    result = products(shifts, facts, proj, greater)
    core = core[None]
    first = 0
    for k, size in enumerate(sizes[:-1]):
        if k + 2 < len(sizes):
            pieces[k + 2], result = lax.optimization_barrier((pieces[k + 2], result))
            far.append(lax.ppermute(pieces[k + 2], "energy", up))
        result = products(shifts, facts, proj, far[k], offset=first, before=result)
        first += size
    sums = []
    for group in range(GROUPS):
        keep, send = products(
            shifts, facts, proj, far[-1], offset=first, before=result, core=core, group=group
        )
        sums.append(reduced(keep, send, planes, share))
    scale = 1.0 / math.sqrt(2.0 * orbitals * total)
    summed = jnp.concatenate(sums, 0) * scale
    summed = jnp.transpose(summed, (1, 0, 2))
    return summed.reshape(share, photons, 2, orbitals)


def solution(mesh):
    placed = (
        P(("dom", "energy"), None, None, None),
        P(("dom", "energy"), None, None, None),
        P(),
        P(),
        P("dom"),
    )
    return jax.shard_map(
        on_device,
        mesh=mesh,
        in_specs=placed,
        out_specs=P(("dom", "energy"), None, None, None),
        check_vma=False,
    )
```

```python
import functools
import math

import jax
import jax.numpy as jnp
from jax import lax
from jax.experimental import pallas as pl
from jax.experimental.pallas import tpu as pltpu
from jax.sharding import PartitionSpec as P

STEP = 8
WIDE = 16
PAIR = 2
GROUPS = 1
PARTS = (16, 8, 6, 2)
MIB = 1 << 20


def rotated(real, imag):
    top = jnp.concatenate([real, imag], 1)
    bottom = jnp.concatenate([-imag, real], 1)
    return jnp.concatenate([top, bottom], 0)


def cut_kernel(first, sizes, source_ref, *refs):
    sems = refs[-1]
    copies = []
    for k, size in enumerate(sizes):
        copies.append(
            pltpu.make_async_copy(source_ref.at[pl.ds(first, size)], refs[k], sems.at[k])
        )
        copies[-1].start()
        first += size
    for copy in copies:
        copy.wait()


def cut(blocks, first, sizes, limit):
    return pl.pallas_call(
        functools.partial(cut_kernel, first, sizes),
        out_shape=[pltpu.VMEM((size,) + blocks.shape[1:], blocks.dtype) for size in sizes],
        in_specs=[pl.BlockSpec(memory_space=pl.ANY)],
        out_specs=[pl.BlockSpec(memory_space=pltpu.VMEM)] * len(sizes),
        scratch_shapes=[pltpu.SemaphoreType.DMA((len(sizes),))],
        compiler_params=pltpu.CompilerParams(vmem_limit_bytes=limit * MIB),
    )(blocks)


def project_blocks(left, right, lesser_ref, out_ref):
    count, rows, width = out_ref.shape
    inner = [
        jnp.dot(
            left,
            rotated(lesser_ref[u, 0], lesser_ref[u, 1]),
            preferred_element_type=jnp.float32,
        )
        for u in range(count)
    ]
    inner = jnp.concatenate(inner, 0)
    high = inner.astype(jnp.bfloat16)
    low = (inner - high.astype(jnp.float32)).astype(jnp.bfloat16)
    outer = jnp.dot(high, right, preferred_element_type=jnp.float32)
    outer += jnp.dot(low, right, preferred_element_type=jnp.float32)
    out_ref[...] = outer.astype(jnp.bfloat16).reshape(count, rows, width)


def project_kernel(steps, left_ref, right_ref, own_ref, other_ref, out_ref):
    t = pl.program_id(0)

    @pl.when(t < steps)
    def _():
        project_blocks(left_ref[...], right_ref[...], own_ref, out_ref)

    @pl.when((t >= steps) & (t < 2 * steps))
    def _():
        project_blocks(left_ref[...], right_ref[...], other_ref, out_ref)

    @pl.when(t == 2 * steps)
    def _():
        out_ref[...] = jnp.zeros_like(out_ref)


def project(left, right, own, other):
    energies, _, orbitals, _ = own.shape
    width = 2 * orbitals
    steps = energies // WIDE
    slots = 2 * energies + WIDE
    return pl.pallas_call(
        functools.partial(project_kernel, steps),
        out_shape=jax.ShapeDtypeStruct((slots, orbitals, width), jnp.bfloat16),
        grid=(2 * steps + 1,),
        in_specs=[
            pl.BlockSpec((orbitals, width), lambda t: (0, 0)),
            pl.BlockSpec((width, width), lambda t: (0, 0)),
            pl.BlockSpec(
                (WIDE, 2, orbitals, orbitals), lambda t: (jnp.minimum(t, steps - 1), 0, 0, 0)
            ),
            pl.BlockSpec(
                (WIDE, 2, orbitals, orbitals),
                lambda t: (jnp.clip(t - steps, 0, steps - 1), 0, 0, 0),
            ),
        ],
        out_specs=pl.BlockSpec((WIDE, orbitals, width), lambda t: (t, 0, 0)),
        compiler_params=pltpu.CompilerParams(vmem_limit_bytes=16 * MIB),
    )(left, right, own, other)


def pair_place(shift, offset, far, facts_ref, zero_place):
    low, high, base, limit, e_dev = (facts_ref[i] for i in range(5))
    reach = offset + shift
    energy = base + offset
    if far:
        energy = energy - 2 * e_dev
    met = reach >= limit if far else reach < limit
    met = met & (energy >= low) & (energy + shift < high)
    if far:
        reach = jnp.where(reach >= 2 * e_dev, reach - 2 * e_dev, reach)
    return jnp.where(met, reach, zero_place)


def add_products(shifts_ref, facts_ref, proj_ref, green_ref, total_ref, start, far, offset):
    step = green_ref.shape[0]
    first = pl.program_id(0) * step + offset
    photons, rows, width = total_ref.shape
    zero_place = proj_ref.shape[0] - 1
    for w in range(0, photons, PAIR):
        shifts = [shifts_ref[start + w + v] for v in range(PAIR)]
        total = total_ref[w : w + PAIR].reshape(PAIR * rows, width)
        for u in range(step):
            places = [pair_place(shift, first + u, far, facts_ref, zero_place) for shift in shifts]
            left = jnp.concatenate([proj_ref[place] for place in places], 0)
            right = rotated(green_ref[u, 0], green_ref[u, 1])
            total += jnp.dot(left, right, preferred_element_type=jnp.float32)
        total_ref[w : w + PAIR] = total.reshape(PAIR, rows, width)


def near_kernel(shifts_ref, facts_ref, proj_ref, green_ref, total_ref):
    @pl.when(pl.program_id(0) == 0)
    def _():
        total_ref[...] = jnp.zeros_like(total_ref)

    add_products(shifts_ref, facts_ref, proj_ref, green_ref, total_ref, 0, False, 0)


def far_kernel(offset, shifts_ref, facts_ref, proj_ref, green_ref, before_ref, total_ref):
    @pl.when(pl.program_id(0) == 0)
    def _():
        total_ref[...] = before_ref[...]

    add_products(shifts_ref, facts_ref, proj_ref, green_ref, total_ref, 0, True, offset)


def last_kernel(
    start,
    offset,
    shifts_ref,
    facts_ref,
    core_ref,
    proj_ref,
    green_ref,
    before_ref,
    keep_ref,
    send_ref,
    total_ref,
):
    @pl.when(pl.program_id(0) == 0)
    def _():
        total_ref[...] = before_ref[...]

    add_products(shifts_ref, facts_ref, proj_ref, green_ref, total_ref, start, True, offset)

    @pl.when(pl.program_id(0) == pl.num_programs(0) - 1)
    def _():
        half = keep_ref.shape[1]
        core = core_ref[0]
        own = pl.multiple_of(core * half, half)
        other = pl.multiple_of((1 - core) * half, half)
        keep_ref[...] = total_ref[:, pl.ds(own, half), :]
        send_ref[...] = total_ref[:, pl.ds(other, half), :].astype(send_ref.dtype)


def products(shifts, facts, proj, green, offset=0, before=None, core=None, group=0):
    slots, rows, width = proj.shape
    energies, _, orbitals, _ = green.shape
    step = math.gcd(STEP, energies)
    photons = shifts.shape[0]
    smem = pl.BlockSpec(memory_space=pltpu.SMEM)
    if core is not None:
        photons //= GROUPS
    block = (photons, rows, width)
    operands, specs = [shifts, facts], [smem, smem]
    if core is not None:
        operands.append(core)
        specs.append(smem)
    operands += [proj, green]
    specs += [
        pl.BlockSpec((slots, rows, width), lambda t: (0, 0, 0), pipeline_mode=pl.Buffered(1)),
        pl.BlockSpec((step, 2, orbitals, orbitals), lambda t: (t, 0, 0, 0)),
    ]
    if before is not None:
        operands.append(before)
        specs.append(
            pl.BlockSpec(block, lambda t: (group, 0, 0), pipeline_mode=pl.Buffered(1))
        )
    scratch = []
    if core is not None:
        half = (photons, rows // 2, width)
        kernel = functools.partial(last_kernel, group * photons, offset)
        out_specs = [pl.BlockSpec(half, lambda t: (0, 0, 0))] * 2
        out_shape = [
            jax.ShapeDtypeStruct(half, jnp.float32),
            jax.ShapeDtypeStruct(half, jnp.bfloat16),
        ]
        scratch = [pltpu.VMEM(block, jnp.float32)]
    else:
        kernel = near_kernel if before is None else functools.partial(far_kernel, offset)
        out_specs = pl.BlockSpec(block, lambda t: (0, 0, 0))
        out_shape = jax.ShapeDtypeStruct(block, jnp.float32)
    return pl.pallas_call(
        kernel,
        out_shape=out_shape,
        grid=(energies // step,),
        in_specs=specs,
        out_specs=out_specs,
        scratch_shapes=scratch,
        compiler_params=pltpu.CompilerParams(vmem_limit_bytes=24 * MIB),
    )(*operands)


def pick(blocks, place):
    return lax.dynamic_index_in_dim(blocks, place, 0, keepdims=False)


def reduced(keep, send, planes, share):
    devices = 4 * planes
    index = lax.axis_index("energy")
    plane, chip = index // 4, (index // 2) % 2
    photons, half, width = keep.shape
    rows = half // 2

    def over_cores(chip):
        mine = lax.dynamic_slice_in_dim(keep, chip * rows, rows, 1)
        part = lax.dynamic_slice_in_dim(send, chip * rows, rows, 1)
        got = lax.ppermute(part, "energy", [(i, i ^ 1) for i in range(devices)])
        both = (mine + got.astype(jnp.float32)).reshape(photons, planes, share, width)
        return jnp.transpose(both, (1, 0, 2, 3))

    theirs = over_cores(1 - chip)
    keep = lax.optimization_barrier(keep)
    mine = over_cores(chip)
    steps = sorted(range(1, planes), key=lambda k: -min(k, planes - k)) + [0]
    sums = []
    for part in (steps[: planes // 2], steps[planes // 2 :]):
        at = [(plane + step) % planes for step in part]
        send = jnp.stack([pick(theirs, k) for k in at]).astype(jnp.bfloat16)
        got = lax.ppermute(send, "energy", [(i, i ^ 2) for i in range(devices)])
        sums += [pick(mine, k) + got[n].astype(jnp.float32) for n, k in enumerate(at)]
        mine = lax.optimization_barrier(mine)
    total = sums[-1]
    for step, block in zip(steps[:-1], sums):
        route = [(i, (i + 4 * step) % devices) for i in range(devices)]
        total = total + lax.ppermute(block.astype(jnp.bfloat16), "energy", route).astype(
            jnp.float32
        )
    return total


def on_device(lesser, greater, dipole, shifts, window):
    e_dev, _, orbitals, _ = lesser.shape
    photons = shifts.shape[0]
    devices = lax.axis_size("energy")
    index = lax.axis_index("energy")
    core = index % 2
    share = orbitals // devices
    total = e_dev * devices

    up = [(i, i + 2) for i in range(devices - 2)]
    across = [(i, i ^ 1) for i in range(devices)]
    sizes = [e_dev * part // 32 for part in PARTS]
    pieces = list(cut(greater, 0, sizes[:1], 50))
    far = [lax.ppermute(pieces[0], "energy", up)]

    planes = devices // 4
    rows = dipole.reshape(2, planes, 2, 2, share, orbitals)
    rows = jnp.transpose(rows, (0, 3, 2, 1, 4, 5)).reshape(2, orbitals, orbitals)
    left = jnp.concatenate([rows[0], rows[1]], 1)
    real, imag = dipole[0].T, dipole[1].T
    right = jnp.concatenate(
        [jnp.concatenate([real, -imag], 1), jnp.concatenate([imag, real], 1)], 0
    )
    proj = project(left, right, lesser, lax.ppermute(lesser, "energy", across))

    rest, proj = lax.optimization_barrier((greater, proj))
    pieces += list(cut(rest, sizes[0], sizes[1:], 8))
    far.append(lax.ppermute(pieces[1], "energy", up))

    limit = jnp.where(core == 0, 2 * e_dev, e_dev)
    facts = jnp.stack([window[0], window[1], index * e_dev, limit, jnp.int32(e_dev)])
    facts = facts.astype(jnp.int32)
    result = products(shifts, facts, proj, greater)
    core = core[None]
    first = 0
    for k, size in enumerate(sizes[:-1]):
        if k + 2 < len(sizes):
            pieces[k + 2], result = lax.optimization_barrier((pieces[k + 2], result))
            far.append(lax.ppermute(pieces[k + 2], "energy", up))
        result = products(shifts, facts, proj, far[k], offset=first, before=result)
        first += size
    sums = []
    for group in range(GROUPS):
        keep, send = products(
            shifts, facts, proj, far[-1], offset=first, before=result, core=core, group=group
        )
        sums.append(reduced(keep, send, planes, share))
    scale = 1.0 / math.sqrt(2.0 * orbitals * total)
    summed = jnp.concatenate(sums, 0) * scale
    summed = jnp.transpose(summed, (1, 0, 2))
    return summed.reshape(share, photons, 2, orbitals)


def solution(mesh):
    placed = (
        P(("dom", "energy"), None, None, None),
        P(("dom", "energy"), None, None, None),
        P(),
        P(),
        P("dom"),
    )
    return jax.shard_map(
        on_device,
        mesh=mesh,
        in_specs=placed,
        out_specs=P(("dom", "energy"), None, None, None),
        check_vma=False,
    )
```

```python
import functools
import math

import jax
import jax.numpy as jnp
from jax import lax
from jax.experimental import pallas as pl
from jax.experimental.pallas import tpu as pltpu
from jax.sharding import PartitionSpec as P

STEP = 8
WIDE = 16
PAIR = 2
GROUPS = 1
PARTS = (16, 8, 6, 2)
MIB = 1 << 20


def rotated(real, imag):
    top = jnp.concatenate([real, imag], 1)
    bottom = jnp.concatenate([-imag, real], 1)
    return jnp.concatenate([top, bottom], 0)


def cut_kernel(first, sizes, source_ref, *refs):
    sems = refs[-1]
    copies = []
    for k, size in enumerate(sizes):
        copies.append(
            pltpu.make_async_copy(source_ref.at[pl.ds(first, size)], refs[k], sems.at[k])
        )
        copies[-1].start()
        first += size
    for copy in copies:
        copy.wait()


def cut(blocks, first, sizes, limit):
    return pl.pallas_call(
        functools.partial(cut_kernel, first, sizes),
        out_shape=[pltpu.VMEM((size,) + blocks.shape[1:], blocks.dtype) for size in sizes],
        in_specs=[pl.BlockSpec(memory_space=pl.ANY)],
        out_specs=[pl.BlockSpec(memory_space=pltpu.VMEM)] * len(sizes),
        scratch_shapes=[pltpu.SemaphoreType.DMA((len(sizes),))],
        compiler_params=pltpu.CompilerParams(vmem_limit_bytes=limit * MIB),
    )(blocks)


def project_blocks(left, right, lesser_ref, out_ref):
    count, rows, width = out_ref.shape
    inner = [
        jnp.dot(
            left,
            rotated(lesser_ref[u, 0], lesser_ref[u, 1]),
            preferred_element_type=jnp.float32,
        )
        for u in range(count)
    ]
    inner = jnp.concatenate(inner, 0)
    high = inner.astype(jnp.bfloat16)
    low = (inner - high.astype(jnp.float32)).astype(jnp.bfloat16)
    outer = jnp.dot(high, right, preferred_element_type=jnp.float32)
    outer += jnp.dot(low, right, preferred_element_type=jnp.float32)
    out_ref[...] = outer.astype(jnp.bfloat16).reshape(count, rows, width)


def project_kernel(steps, left_ref, right_ref, own_ref, other_ref, out_ref):
    t = pl.program_id(0)

    @pl.when(t < steps)
    def _():
        project_blocks(left_ref[...], right_ref[...], own_ref, out_ref)

    @pl.when((t >= steps) & (t < 2 * steps))
    def _():
        project_blocks(left_ref[...], right_ref[...], other_ref, out_ref)

    @pl.when(t == 2 * steps)
    def _():
        out_ref[...] = jnp.zeros_like(out_ref)


def project(left, right, own, other):
    energies, _, orbitals, _ = own.shape
    width = 2 * orbitals
    steps = energies // WIDE
    slots = 2 * energies + WIDE
    return pl.pallas_call(
        functools.partial(project_kernel, steps),
        out_shape=jax.ShapeDtypeStruct((slots, orbitals, width), jnp.bfloat16),
        grid=(2 * steps + 1,),
        in_specs=[
            pl.BlockSpec((orbitals, width), lambda t: (0, 0)),
            pl.BlockSpec((width, width), lambda t: (0, 0)),
            pl.BlockSpec(
                (WIDE, 2, orbitals, orbitals), lambda t: (jnp.minimum(t, steps - 1), 0, 0, 0)
            ),
            pl.BlockSpec(
                (WIDE, 2, orbitals, orbitals),
                lambda t: (jnp.clip(t - steps, 0, steps - 1), 0, 0, 0),
            ),
        ],
        out_specs=pl.BlockSpec((WIDE, orbitals, width), lambda t: (t, 0, 0)),
        compiler_params=pltpu.CompilerParams(vmem_limit_bytes=16 * MIB),
    )(left, right, own, other)


def pair_place(shift, offset, far, facts_ref, zero_place):
    low, high, base, limit, e_dev = (facts_ref[i] for i in range(5))
    reach = offset + shift
    energy = base + offset
    if far:
        energy = energy - 2 * e_dev
    met = reach >= limit if far else reach < limit
    met = met & (energy >= low) & (energy + shift < high)
    if far:
        reach = jnp.where(reach >= 2 * e_dev, reach - 2 * e_dev, reach)
    return jnp.where(met, reach, zero_place)


def add_products(shifts_ref, facts_ref, proj_ref, green_ref, total_ref, start, far, offset):
    step = green_ref.shape[0]
    first = pl.program_id(0) * step + offset
    photons, rows, width = total_ref.shape
    zero_place = proj_ref.shape[0] - 1
    for w in range(0, photons, PAIR):
        shifts = [shifts_ref[start + w + v] for v in range(PAIR)]
        total = total_ref[w : w + PAIR].reshape(PAIR * rows, width)
        for u in range(step):
            places = [pair_place(shift, first + u, far, facts_ref, zero_place) for shift in shifts]
            left = jnp.concatenate([proj_ref[place] for place in places], 0)
            right = rotated(green_ref[u, 0], green_ref[u, 1])
            total += jnp.dot(left, right, preferred_element_type=jnp.float32)
        total_ref[w : w + PAIR] = total.reshape(PAIR, rows, width)


def near_kernel(shifts_ref, facts_ref, proj_ref, green_ref, total_ref):
    @pl.when(pl.program_id(0) == 0)
    def _():
        total_ref[...] = jnp.zeros_like(total_ref)

    add_products(shifts_ref, facts_ref, proj_ref, green_ref, total_ref, 0, False, 0)


def far_kernel(offset, shifts_ref, facts_ref, proj_ref, green_ref, before_ref, total_ref):
    @pl.when(pl.program_id(0) == 0)
    def _():
        total_ref[...] = before_ref[...]

    add_products(shifts_ref, facts_ref, proj_ref, green_ref, total_ref, 0, True, offset)


def last_kernel(
    start,
    offset,
    shifts_ref,
    facts_ref,
    core_ref,
    proj_ref,
    green_ref,
    before_ref,
    keep_ref,
    send_ref,
    total_ref,
):
    @pl.when(pl.program_id(0) == 0)
    def _():
        total_ref[...] = before_ref[...]

    add_products(shifts_ref, facts_ref, proj_ref, green_ref, total_ref, start, True, offset)

    @pl.when(pl.program_id(0) == pl.num_programs(0) - 1)
    def _():
        half = keep_ref.shape[1]
        core = core_ref[0]
        own = pl.multiple_of(core * half, half)
        other = pl.multiple_of((1 - core) * half, half)
        keep_ref[...] = total_ref[:, pl.ds(own, half), :]
        send_ref[...] = total_ref[:, pl.ds(other, half), :].astype(send_ref.dtype)


def products(shifts, facts, proj, green, offset=0, before=None, core=None, group=0):
    slots, rows, width = proj.shape
    energies, _, orbitals, _ = green.shape
    step = math.gcd(STEP, energies)
    photons = shifts.shape[0]
    smem = pl.BlockSpec(memory_space=pltpu.SMEM)
    if core is not None:
        photons //= GROUPS
    block = (photons, rows, width)
    operands, specs = [shifts, facts], [smem, smem]
    if core is not None:
        operands.append(core)
        specs.append(smem)
    operands += [proj, green]
    specs += [
        pl.BlockSpec((slots, rows, width), lambda t: (0, 0, 0), pipeline_mode=pl.Buffered(1)),
        pl.BlockSpec((step, 2, orbitals, orbitals), lambda t: (t, 0, 0, 0)),
    ]
    if before is not None:
        operands.append(before)
        specs.append(
            pl.BlockSpec(block, lambda t: (group, 0, 0), pipeline_mode=pl.Buffered(1))
        )
    scratch = []
    if core is not None:
        half = (photons, rows // 2, width)
        kernel = functools.partial(last_kernel, group * photons, offset)
        out_specs = [pl.BlockSpec(half, lambda t: (0, 0, 0))] * 2
        out_shape = [
            jax.ShapeDtypeStruct(half, jnp.float32),
            jax.ShapeDtypeStruct(half, jnp.bfloat16),
        ]
        scratch = [pltpu.VMEM(block, jnp.float32)]
    else:
        kernel = near_kernel if before is None else functools.partial(far_kernel, offset)
        out_specs = pl.BlockSpec(block, lambda t: (0, 0, 0))
        out_shape = jax.ShapeDtypeStruct(block, jnp.float32)
    return pl.pallas_call(
        kernel,
        out_shape=out_shape,
        grid=(energies // step,),
        in_specs=specs,
        out_specs=out_specs,
        scratch_shapes=scratch,
        compiler_params=pltpu.CompilerParams(vmem_limit_bytes=24 * MIB),
    )(*operands)


def pick(blocks, place):
    return lax.dynamic_index_in_dim(blocks, place, 0, keepdims=False)


def reduced(keep, send, planes, share):
    devices = 4 * planes
    index = lax.axis_index("energy")
    plane, chip = index // 4, (index // 2) % 2
    photons, half, width = keep.shape
    got = lax.ppermute(send, "energy", [(i, i ^ 1) for i in range(devices)])
    both = keep + got.astype(jnp.float32)
    both = both.reshape(photons, 2, planes, share, width)
    both = jnp.transpose(both, (1, 2, 0, 3, 4))
    theirs, mine = pick(both, 1 - chip), pick(both, chip)
    steps = sorted(range(1, planes), key=lambda k: -min(k, planes - k)) + [0]
    sums = []
    for part in (steps[: planes // 2], steps[planes // 2 :]):
        at = [(plane + step) % planes for step in part]
        send = jnp.stack([pick(theirs, k) for k in at]).astype(jnp.bfloat16)
        got = lax.ppermute(send, "energy", [(i, i ^ 2) for i in range(devices)])
        sums += [pick(mine, k) + got[n].astype(jnp.float32) for n, k in enumerate(at)]
        mine = lax.optimization_barrier(mine)
    total = sums[-1]
    for step, block in zip(steps[:-1], sums):
        route = [(i, (i + 4 * step) % devices) for i in range(devices)]
        total = total + lax.ppermute(block.astype(jnp.bfloat16), "energy", route).astype(
            jnp.float32
        )
    return total


def on_device(lesser, greater, dipole, shifts, window):
    e_dev, _, orbitals, _ = lesser.shape
    photons = shifts.shape[0]
    devices = lax.axis_size("energy")
    index = lax.axis_index("energy")
    core = index % 2
    share = orbitals // devices
    total = e_dev * devices

    up = [(i, i + 2) for i in range(devices - 2)]
    across = [(i, i ^ 1) for i in range(devices)]
    sizes = [e_dev * part // 32 for part in PARTS]
    pieces = list(cut(greater, 0, sizes[:1], 50))
    far = [lax.ppermute(pieces[0], "energy", up)]

    planes = devices // 4
    rows = dipole.reshape(2, planes, 2, 2, share, orbitals)
    rows = jnp.transpose(rows, (0, 3, 2, 1, 4, 5)).reshape(2, orbitals, orbitals)
    left = jnp.concatenate([rows[0], rows[1]], 1)
    real, imag = dipole[0].T, dipole[1].T
    right = jnp.concatenate(
        [jnp.concatenate([real, -imag], 1), jnp.concatenate([imag, real], 1)], 0
    )
    proj = project(left, right, lesser, lax.ppermute(lesser, "energy", across))

    limit = jnp.where(core == 0, 2 * e_dev, e_dev)
    facts = jnp.stack([window[0], window[1], index * e_dev, limit, jnp.int32(e_dev)])
    facts = facts.astype(jnp.int32)
    facts = facts + proj[-1, 0, 0].astype(jnp.int32)
    rest, facts = lax.optimization_barrier((greater, facts))
    pieces += list(cut(rest, sizes[0], sizes[1:], 8))
    far.append(lax.ppermute(pieces[1], "energy", up))

    result = products(shifts, facts, proj, greater)
    core = core[None]
    first = 0
    for k, size in enumerate(sizes[:-1]):
        if k + 2 < len(sizes):
            pieces[k + 2], result = lax.optimization_barrier((pieces[k + 2], result))
            far.append(lax.ppermute(pieces[k + 2], "energy", up))
        result = products(shifts, facts, proj, far[k], offset=first, before=result)
        first += size
    sums = []
    for group in range(GROUPS):
        keep, send = products(
            shifts, facts, proj, far[-1], offset=first, before=result, core=core, group=group
        )
        sums.append(reduced(keep, send, planes, share))
    scale = 1.0 / math.sqrt(2.0 * orbitals * total)
    summed = jnp.concatenate(sums, 0) * scale
    summed = jnp.transpose(summed, (1, 0, 2))
    return summed.reshape(share, photons, 2, orbitals)


def solution(mesh):
    placed = (
        P(("dom", "energy"), None, None, None),
        P(("dom", "energy"), None, None, None),
        P(),
        P(),
        P("dom"),
    )
    return jax.shard_map(
        on_device,
        mesh=mesh,
        in_specs=placed,
        out_specs=P(("dom", "energy"), None, None, None),
        check_vma=False,
    )
```

```python
import functools
import math

import jax
import jax.numpy as jnp
from jax import lax
from jax.experimental import pallas as pl
from jax.experimental.pallas import tpu as pltpu
from jax.sharding import PartitionSpec as P

STEP = 16
WIDE = 16
PAIR = 2
GROUPS = 1
PARTS = (16, 8, 6, 2)
MIB = 1 << 20


def rotated(real, imag):
    top = jnp.concatenate([real, imag], 1)
    bottom = jnp.concatenate([-imag, real], 1)
    return jnp.concatenate([top, bottom], 0)


def cut_kernel(first, sizes, source_ref, *refs):
    sems = refs[-1]
    copies = []
    for k, size in enumerate(sizes):
        copies.append(
            pltpu.make_async_copy(source_ref.at[pl.ds(first, size)], refs[k], sems.at[k])
        )
        copies[-1].start()
        first += size
    for copy in copies:
        copy.wait()


def cut(blocks, first, sizes, limit):
    return pl.pallas_call(
        functools.partial(cut_kernel, first, sizes),
        out_shape=[pltpu.VMEM((size,) + blocks.shape[1:], blocks.dtype) for size in sizes],
        in_specs=[pl.BlockSpec(memory_space=pl.ANY)],
        out_specs=[pl.BlockSpec(memory_space=pltpu.VMEM)] * len(sizes),
        scratch_shapes=[pltpu.SemaphoreType.DMA((len(sizes),))],
        compiler_params=pltpu.CompilerParams(vmem_limit_bytes=limit * MIB),
    )(blocks)


def project_blocks(left, right, lesser_ref, out_ref):
    count, rows, width = out_ref.shape
    inner = [
        jnp.dot(
            left,
            rotated(lesser_ref[u, 0], lesser_ref[u, 1]),
            preferred_element_type=jnp.float32,
        )
        for u in range(count)
    ]
    inner = jnp.concatenate(inner, 0)
    high = inner.astype(jnp.bfloat16)
    low = (inner - high.astype(jnp.float32)).astype(jnp.bfloat16)
    outer = jnp.dot(high, right, preferred_element_type=jnp.float32)
    outer += jnp.dot(low, right, preferred_element_type=jnp.float32)
    out_ref[...] = outer.astype(jnp.bfloat16).reshape(count, rows, width)


def project_kernel(steps, left_ref, right_ref, own_ref, other_ref, out_ref):
    t = pl.program_id(0)

    @pl.when(t < steps)
    def _():
        project_blocks(left_ref[...], right_ref[...], own_ref, out_ref)

    @pl.when((t >= steps) & (t < 2 * steps))
    def _():
        project_blocks(left_ref[...], right_ref[...], other_ref, out_ref)

    @pl.when(t == 2 * steps)
    def _():
        out_ref[...] = jnp.zeros_like(out_ref)


def project(left, right, own, other):
    energies, _, orbitals, _ = own.shape
    width = 2 * orbitals
    steps = energies // WIDE
    slots = 2 * energies + WIDE
    return pl.pallas_call(
        functools.partial(project_kernel, steps),
        out_shape=jax.ShapeDtypeStruct((slots, orbitals, width), jnp.bfloat16),
        grid=(2 * steps + 1,),
        in_specs=[
            pl.BlockSpec((orbitals, width), lambda t: (0, 0)),
            pl.BlockSpec((width, width), lambda t: (0, 0)),
            pl.BlockSpec(
                (WIDE, 2, orbitals, orbitals), lambda t: (jnp.minimum(t, steps - 1), 0, 0, 0)
            ),
            pl.BlockSpec(
                (WIDE, 2, orbitals, orbitals),
                lambda t: (jnp.clip(t - steps, 0, steps - 1), 0, 0, 0),
            ),
        ],
        out_specs=pl.BlockSpec((WIDE, orbitals, width), lambda t: (t, 0, 0)),
        compiler_params=pltpu.CompilerParams(vmem_limit_bytes=16 * MIB),
    )(left, right, own, other)


def pair_place(shift, offset, far, facts_ref, zero_place):
    low, high, base, limit, e_dev = (facts_ref[i] for i in range(5))
    reach = offset + shift
    energy = base + offset
    if far:
        energy = energy - 2 * e_dev
    met = reach >= limit if far else reach < limit
    met = met & (energy >= low) & (energy + shift < high)
    if far:
        reach = jnp.where(reach >= 2 * e_dev, reach - 2 * e_dev, reach)
    return jnp.where(met, reach, zero_place)


def add_products(shifts_ref, facts_ref, proj_ref, green_ref, total_ref, start, far, offset):
    step = green_ref.shape[0]
    first = pl.program_id(0) * step + offset
    photons, rows, width = total_ref.shape
    zero_place = proj_ref.shape[0] - 1
    for w in range(0, photons, PAIR):
        shifts = [shifts_ref[start + w + v] for v in range(PAIR)]
        total = total_ref[w : w + PAIR].reshape(PAIR * rows, width)
        for u in range(step):
            places = [pair_place(shift, first + u, far, facts_ref, zero_place) for shift in shifts]
            left = jnp.concatenate([proj_ref[place] for place in places], 0)
            right = rotated(green_ref[u, 0], green_ref[u, 1])
            total += jnp.dot(left, right, preferred_element_type=jnp.float32)
        total_ref[w : w + PAIR] = total.reshape(PAIR, rows, width)


def near_kernel(shifts_ref, facts_ref, proj_ref, green_ref, total_ref):
    @pl.when(pl.program_id(0) == 0)
    def _():
        total_ref[...] = jnp.zeros_like(total_ref)

    add_products(shifts_ref, facts_ref, proj_ref, green_ref, total_ref, 0, False, 0)


def far_kernel(offset, shifts_ref, facts_ref, proj_ref, green_ref, before_ref, total_ref):
    @pl.when(pl.program_id(0) == 0)
    def _():
        total_ref[...] = before_ref[...]

    add_products(shifts_ref, facts_ref, proj_ref, green_ref, total_ref, 0, True, offset)


def last_kernel(
    start,
    offset,
    shifts_ref,
    facts_ref,
    core_ref,
    proj_ref,
    green_ref,
    before_ref,
    keep_ref,
    send_ref,
    total_ref,
):
    @pl.when(pl.program_id(0) == 0)
    def _():
        total_ref[...] = before_ref[...]

    add_products(shifts_ref, facts_ref, proj_ref, green_ref, total_ref, start, True, offset)

    @pl.when(pl.program_id(0) == pl.num_programs(0) - 1)
    def _():
        half = keep_ref.shape[1]
        core = core_ref[0]
        own = pl.multiple_of(core * half, half)
        other = pl.multiple_of((1 - core) * half, half)
        keep_ref[...] = total_ref[:, pl.ds(own, half), :]
        send_ref[...] = total_ref[:, pl.ds(other, half), :].astype(send_ref.dtype)


def products(shifts, facts, proj, green, offset=0, before=None, core=None, group=0):
    slots, rows, width = proj.shape
    energies, _, orbitals, _ = green.shape
    step = math.gcd(STEP, energies)
    photons = shifts.shape[0]
    smem = pl.BlockSpec(memory_space=pltpu.SMEM)
    if core is not None:
        photons //= GROUPS
    block = (photons, rows, width)
    operands, specs = [shifts, facts], [smem, smem]
    if core is not None:
        operands.append(core)
        specs.append(smem)
    operands += [proj, green]
    specs += [
        pl.BlockSpec((slots, rows, width), lambda t: (0, 0, 0), pipeline_mode=pl.Buffered(1)),
        pl.BlockSpec((step, 2, orbitals, orbitals), lambda t: (t, 0, 0, 0)),
    ]
    if before is not None:
        operands.append(before)
        specs.append(
            pl.BlockSpec(block, lambda t: (group, 0, 0), pipeline_mode=pl.Buffered(1))
        )
    scratch = []
    if core is not None:
        half = (photons, rows // 2, width)
        kernel = functools.partial(last_kernel, group * photons, offset)
        out_specs = [pl.BlockSpec(half, lambda t: (0, 0, 0))] * 2
        out_shape = [
            jax.ShapeDtypeStruct(half, jnp.float32),
            jax.ShapeDtypeStruct(half, jnp.bfloat16),
        ]
        scratch = [pltpu.VMEM(block, jnp.float32)]
    else:
        kernel = near_kernel if before is None else functools.partial(far_kernel, offset)
        out_specs = pl.BlockSpec(block, lambda t: (0, 0, 0))
        out_shape = jax.ShapeDtypeStruct(block, jnp.float32)
    return pl.pallas_call(
        kernel,
        out_shape=out_shape,
        grid=(energies // step,),
        in_specs=specs,
        out_specs=out_specs,
        scratch_shapes=scratch,
        compiler_params=pltpu.CompilerParams(vmem_limit_bytes=24 * MIB),
    )(*operands)


def pick(blocks, place):
    return lax.dynamic_index_in_dim(blocks, place, 0, keepdims=False)


def reduced(keep, send, planes, share):
    devices = 4 * planes
    index = lax.axis_index("energy")
    plane, chip = index // 4, (index // 2) % 2
    photons, half, width = keep.shape
    got = lax.ppermute(send, "energy", [(i, i ^ 1) for i in range(devices)])
    both = keep + got.astype(jnp.float32)
    both = both.reshape(photons, 2, planes, share, width)
    both = jnp.transpose(both, (1, 2, 0, 3, 4))
    theirs, mine = pick(both, 1 - chip), pick(both, chip)
    steps = sorted(range(1, planes), key=lambda k: -min(k, planes - k)) + [0]
    sums = []
    for part in (steps[: planes // 2], steps[planes // 2 :]):
        at = [(plane + step) % planes for step in part]
        send = jnp.stack([pick(theirs, k) for k in at]).astype(jnp.bfloat16)
        got = lax.ppermute(send, "energy", [(i, i ^ 2) for i in range(devices)])
        sums += [pick(mine, k) + got[n].astype(jnp.float32) for n, k in enumerate(at)]
        mine = lax.optimization_barrier(mine)
    total = sums[-1]
    for step, block in zip(steps[:-1], sums):
        route = [(i, (i + 4 * step) % devices) for i in range(devices)]
        total = total + lax.ppermute(block.astype(jnp.bfloat16), "energy", route).astype(
            jnp.float32
        )
    return total


def on_device(lesser, greater, dipole, shifts, window):
    e_dev, _, orbitals, _ = lesser.shape
    photons = shifts.shape[0]
    devices = lax.axis_size("energy")
    index = lax.axis_index("energy")
    core = index % 2
    share = orbitals // devices
    total = e_dev * devices

    up = [(i, i + 2) for i in range(devices - 2)]
    across = [(i, i ^ 1) for i in range(devices)]
    sizes = [e_dev * part // 32 for part in PARTS]
    pieces = list(cut(greater, 0, sizes[:1], 50))
    far = [lax.ppermute(pieces[0], "energy", up)]

    planes = devices // 4
    rows = dipole.reshape(2, planes, 2, 2, share, orbitals)
    rows = jnp.transpose(rows, (0, 3, 2, 1, 4, 5)).reshape(2, orbitals, orbitals)
    left = jnp.concatenate([rows[0], rows[1]], 1)
    real, imag = dipole[0].T, dipole[1].T
    right = jnp.concatenate(
        [jnp.concatenate([real, -imag], 1), jnp.concatenate([imag, real], 1)], 0
    )
    proj = project(left, right, lesser, lax.ppermute(lesser, "energy", across))

    rest, proj = lax.optimization_barrier((greater, proj))
    pieces += list(cut(rest, sizes[0], sizes[1:], 8))
    far.append(lax.ppermute(pieces[1], "energy", up))

    limit = jnp.where(core == 0, 2 * e_dev, e_dev)
    facts = jnp.stack([window[0], window[1], index * e_dev, limit, jnp.int32(e_dev)])
    facts = facts.astype(jnp.int32)
    result = products(shifts, facts, proj, greater)
    core = core[None]
    first = 0
    for k, size in enumerate(sizes[:-1]):
        if k + 2 < len(sizes):
            pieces[k + 2], result = lax.optimization_barrier((pieces[k + 2], result))
            far.append(lax.ppermute(pieces[k + 2], "energy", up))
        result = products(shifts, facts, proj, far[k], offset=first, before=result)
        first += size
    sums = []
    for group in range(GROUPS):
        keep, send = products(
            shifts, facts, proj, far[-1], offset=first, before=result, core=core, group=group
        )
        sums.append(reduced(keep, send, planes, share))
    scale = 1.0 / math.sqrt(2.0 * orbitals * total)
    summed = jnp.concatenate(sums, 0) * scale
    summed = jnp.transpose(summed, (1, 0, 2))
    return summed.reshape(share, photons, 2, orbitals)


def solution(mesh):
    placed = (
        P(("dom", "energy"), None, None, None),
        P(("dom", "energy"), None, None, None),
        P(),
        P(),
        P("dom"),
    )
    return jax.shard_map(
        on_device,
        mesh=mesh,
        in_specs=placed,
        out_specs=P(("dom", "energy"), None, None, None),
        check_vma=False,
    )
```
